512 devices in a mesh: gx: 32 (over z, core), gy: 16 (over x, y).
Axes of the slice: x: 4, y: 4, z: 16, core: 2. Of those that a mesh axis runs over, the one named last changes fastest.
Arguments:
- adjoint_source: float32 [4, 128, 128, 256], P(None, 'gx', 'gy'), may hold values from -60 to 60, as said below
- labels: int32 [128, 128, 256], P('gx', 'gy'), may hold values from 0 to 2
- bv_mask: int32 [128, 128, 256], P('gx', 'gy'), may hold values 0 or 1
- conduct: bfloat16 [4, 128, 128, 256], P(None, 'gx', 'gy'), may hold values from 0.29882812 to 3
- bv_rate: bfloat16 [3, 128, 128, 256], P(None, 'gx', 'gy'), may hold values from 0.5 to 4
Outputs:
- adjoint: float32 [4, 128, 128, 256], P(None, 'gx', 'gy')
- residual: float32 [4, 128, 128, 256], P(None, 'gx', 'gy')
The draws below stay inside these ranges and needn't reach their ends.
Inputs may be any that keep to these rules, and one draw needn't show every extreme that they name: `adjoint_source`: entries of order one with scales that vary over voxels.
All inputs are finite; a program needn't handle non-finite values. No bound on the sum of `bv_mask` on one device may be relied on, other than what follows from the above.
Results may differ from the reference program's by a relative error of at most 0.029.
Values sent between devices are 32-bit elements; how exact they have to be, the bound alone decides.
No kernel may reach another device: no remote copies, remote signals or barrier semaphores. Data moves between devices by JAX's collectives and lax.ppermute only.
A program may use at most 64 MiB of HBM per device.

```python
import math
import jax
import jax.numpy as jnp

NZ = 256
ITERS = 3
NX = 128
NY = 128


def draw_adjoint_source(key, part):
    key_base = jax.random.fold_in(key, 11)
    key_xs = jax.random.fold_in(key, 12)
    key_ys = jax.random.fold_in(key, 13)
    scale_x = jnp.exp(jax.random.uniform(key_xs, (NX,), jnp.float32, 0.0, math.log(10.0)))
    scale_y = jnp.exp(jax.random.uniform(key_ys, (NY,), jnp.float32, 0.0, math.log(10.0)))
    scale = scale_x[None, :, None, None] * scale_y[None, None, :, None] / 10.0
    base = jnp.clip(jax.random.normal(key_base, (4, NX, NY, NZ), jnp.float32), -6.0, 6.0)
    values = base * scale
    return values.astype(jnp.float32)


def place_ends(result, rng, smallest, high):
    dims = result.shape
    spot = [jax.random.randint(jax.random.fold_in(rng, axis), (), 0, dims[axis]) for axis in range(len(dims))]
    result = result.at[tuple(spot)].set(smallest)
    longest = dims.index(max(dims))
    spot[longest] = (spot[longest] + 1) % dims[longest]
    return result.at[tuple(spot)].set(high)


def block_levels(rng, extent, split, low, largest):
    factor_of, own = 1.0, jax.random.fold_in(rng, 6)
    for dim, blocks in split:
        heights = jnp.exp(jax.random.uniform(jax.random.fold_in(own, dim), (blocks,), jnp.float32, low / len(split), largest / len(split)))
        factor_of = factor_of * jnp.repeat(heights, extent[dim] // blocks).reshape([-1 if axis == dim else 1 for axis in range(len(extent))])
    return factor_of


def setup_inputs(seed: int = 0) -> dict:
    keys = jax.random.split(jax.random.key(seed), 6)
    adjoint_source = draw_adjoint_source(jax.random.fold_in(keys[5], 71), 0)
    labels = place_ends(jax.random.randint(keys[1], (NX, NY, NZ), 0, 3), jax.random.fold_in(keys[1], 1), 0, 2).astype(jnp.int32)
    bv_mask = place_ends((jax.random.randint(keys[2], (NX, NY, NZ), 0, 3) < 1).astype(jnp.int32), jax.random.fold_in(keys[2], 1), 0, 1)
    conduct = jnp.clip(jnp.exp(math.log(3.0) - 2.306499 * jax.random.uniform(keys[3], (4, NX, NY, NZ), jnp.float32) ** block_levels(keys[3], (4, NX, NY, NZ), ((1, 32), (2, 16)), -0.2, 0.2)), 0.29882812, 3.0).astype(jnp.bfloat16)
    bv_rate = jnp.clip(jnp.exp(math.log(4.0) - 2.0794415 * jax.random.uniform(keys[4], (3, NX, NY, NZ), jnp.float32) ** block_levels(keys[4], (3, NX, NY, NZ), ((1, 32), (2, 16)), -0.2, 0.2)), 0.5, 4.0).astype(jnp.bfloat16)
    return dict(adjoint_source=adjoint_source, labels=labels, bv_mask=bv_mask, conduct=conduct, bv_rate=bv_rate)


PHASE = ((1.0, 0.08, 0.08), (1.0, 0.08, 0.08), (0.08, 1.0, 1.0), (0.08, 1.0, 0.08))
SHIFT = (1.0, 0.5, 0.5, 1.0)
WEIGHT = (0.8, 1.0, -1.0, -0.8)
EPS = 1e-12

def cell_conductance(labels, conduct):
    rows = []
    for field in range(4):
        table = PHASE[field]
        base = jnp.where(labels == 0, table[0], jnp.where(labels == 1, table[1], table[2]))
        rows.append(base * conduct[field].astype(jnp.float32))
    return jnp.stack(rows)

def coupling_rows(bv_rate, bv_mask):
    rates = bv_rate.astype(jnp.float32)
    interface = bv_mask.astype(jnp.float32)
    return jnp.stack([rates[2], -rates[0], rates[0], rates[1]]) * interface[None]

def neighbours(padded):
    return [padded[:, 2:, 1:-1, 1:-1], padded[:, :-2, 1:-1, 1:-1], padded[:, 1:-1, 2:, 1:-1], padded[:, 1:-1, :-2, 1:-1], padded[:, 1:-1, 1:-1, 2:], padded[:, 1:-1, 1:-1, :-2]]

def combine(vector, field_pad, cond_pad, kcell, couple):
    total = jnp.zeros_like(vector)
    for cond_side, field_side in zip(neighbours(cond_pad), neighbours(field_pad)):
        total = total + cond_side * (vector - field_side)
    mixed = WEIGHT[0] * vector[0] + WEIGHT[1] * vector[1] + WEIGHT[2] * vector[2] + WEIGHT[3] * vector[3]
    shift = jnp.stack([jnp.full(vector.shape[1:], SHIFT[field], vector.dtype) for field in range(4)])
    return shift * vector + kcell * total + couple * mixed[None]

def least_squares(columns, beta):
    count = len(columns)
    zero = beta * 0.0
    rows = [[columns[col][row] if row <= col + 1 else zero for col in range(count)] for row in range(count + 1)]
    target = [beta] + [zero] * count
    for col in range(count):
        upper = rows[col][col]
        lower = rows[col + 1][col]
        radius = jnp.sqrt(upper * upper + lower * lower)
        cosine = upper / radius
        sine = lower / radius
        for other in range(col, count):
            first = rows[col][other]
            second = rows[col + 1][other]
            rows[col][other] = cosine * first + sine * second
            rows[col + 1][other] = -sine * first + cosine * second
        first = target[col]
        second = target[col + 1]
        target[col] = cosine * first + sine * second
        target[col + 1] = -sine * first + cosine * second
    solved = [zero] * count
    for row in range(count - 1, -1, -1):
        value = target[row]
        for other in range(row + 1, count):
            value = value - rows[row][other] * solved[other]
        solved[row] = value / rows[row][row]
    return solved

def finish(basis, columns, beta):
    count = len(columns)
    solved = least_squares(columns, beta)
    adjoint = solved[0] * basis[0]
    for index in range(1, count):
        adjoint = adjoint + solved[index] * basis[index]
    residual = beta * basis[0]
    for row in range(count + 1):
        value = beta * 0.0
        for col in range(count):
            if row <= col + 1:
                value = value + columns[col][row] * solved[col]
        residual = residual - value * basis[row]
    return (adjoint, residual)

def reference(adjoint_source, labels, bv_mask, conduct, bv_rate):
    kcell = cell_conductance(labels, conduct)
    couple = coupling_rows(bv_rate, bv_mask)
    widths = ((0, 0), (1, 1), (1, 1), (1, 1))
    cond_pad = jnp.pad(kcell, widths)

    def operate(vector):
        return combine(vector, jnp.pad(vector, widths), cond_pad, kcell, couple)
    beta = jnp.sqrt(jnp.sum(adjoint_source * adjoint_source) + EPS)
    basis = [adjoint_source / beta]
    columns = []
    for step in range(ITERS):
        image = operate(basis[step])
        projections = [jnp.sum(image * basis[index]) for index in range(step + 1)]
        work = image
        for index in range(step + 1):
            work = work - projections[index] * basis[index]
        length = jnp.sqrt(jnp.sum(work * work) + EPS)
        columns.append(projections + [length])
        basis.append(work / length)
    return finish(basis, columns, beta)
```

```python
import jax
import jax.numpy as jnp
from jax import lax
from jax.experimental import pallas as pl
from jax.experimental.pallas import tpu as pltpu
from jax.sharding import PartitionSpec as P

PHASE = ((1.0, 0.08, 0.08), (1.0, 0.08, 0.08), (0.08, 1.0, 1.0), (0.08, 1.0, 0.08))
SHIFT = (1.0, 0.5, 0.5, 1.0)
WEIGHT = (0.8, 1.0, -1.0, -0.8)
EPS = 1e-12
F32 = jnp.float32
VMEM = pl.BlockSpec(memory_space=pltpu.VMEM)
TILE = (8, 256)
Y_TILES = 19
X_TILES = 39
PAIRS = [(i, j) for i in range(4) for j in range(i, 4)]


def rows():
    return lax.broadcasted_iota(jnp.int32, TILE, 0)


def roll(tile, by):
    by = by % 8
    return tile if by == 0 else pltpu.roll(tile, by, 0)


def prepare(source, labels, mask, conduct, rate, kcell, couple, to_right, to_left):
    row = rows()
    for x in range(4):
        phase = labels[x]
        for f in range(4):
            t = PHASE[f]
            base = jnp.where(phase == 0, t[0], jnp.where(phase == 1, t[1], t[2]))
            kcell[f, x] = base * conduct[f, x].astype(F32)
        interface = mask[x].astype(F32)
        for f in range(3):
            couple[f, x] = rate[f, x].astype(F32) * interface
    for f in range(8):
        ref = source if f < 4 else kcell
        for k in range(2):
            a, b = ref[f % 4, 2 * k], ref[f % 4, 2 * k + 1]
            to_right[2 * f + k] = jnp.where(row >= 5, a, roll(b, -3))
            to_left[2 * f + k] = jnp.where(row < 3, a, roll(b, 3))
    for f in range(3):
        right, left = couple[f, 0], couple[f, 0]
        for x in range(1, 4):
            right = jnp.where(row >= 8 - 2 * x, right, roll(couple[f, x], -2 * x))
            left = jnp.where(row < 2 * x, left, roll(couple[f, x], 2 * x))
        to_right[16 + f] = right
        to_left[16 + f] = left


def widen(source, kcell, couple, from_left, from_right, rim, crim, to_right, to_left):
    row = rows()
    zero = jnp.zeros(TILE, F32)
    for f in range(8):
        for x in range(4):
            k, b = 2 * f + x // 2, 3 * (x % 2)
            left, right = roll(from_left[k], b), roll(from_right[k], -b)
            rim[f, x] = jnp.where(row < 3, right, jnp.where(row >= 5, left, zero))
    for f in range(3):
        for x in range(4):
            left, right = roll(from_left[16 + f], 2 * x), roll(from_right[16 + f], -2 * x)
            crim[f, x] = jnp.where(row < 2, right, jnp.where(row >= 6, left, zero))
    for out, order in ((to_right, (3, 2, 1)), (to_left, (0, 1, 2))):
        for f in range(8):
            ref = source if f < 4 else kcell
            for d in range(3):
                out[3 * f + d] = ref[f % 4, order[d]]
            out[30 + f] = jnp.where((row == 2) | (row == 3), roll(rim[f, order[1]], 3), rim[f, order[0]])
        for f in range(3):
            for d in range(2):
                out[24 + 2 * f + d] = couple[f, order[d]]
        c = [roll(crim[f, order[0]], 2 * f) for f in range(3)]
        out[38] = jnp.where((row == 0) | (row == 7), c[0], jnp.where(row <= 2, c[1], c[2]))


def krylov(source, kcell, couple, rim, crim, before, after, k1, k2, k3, gram,
           body, edge, cbody, cedge, dbody, dedge, ubody, uedge):
    row = rows()
    lane = lax.broadcasted_iota(jnp.int32, TILE, 1)
    zero = jnp.zeros(TILE, F32)
    for f in range(8):
        ref = source if f < 4 else kcell
        for x in range(4):
            body[f, 3 + x] = ref[f % 4, x]
            edge[f, 3 + x] = rim[f, x]
        for buf, place in ((before, (2, 1, 0)), (after, (7, 8, 9))):
            for d in range(3):
                body[f, place[d]] = buf[3 * f + d]
            t = buf[30 + f]
            edge[f, place[0]] = jnp.where((row < 2) | (row >= 6), t, zero)
            edge[f, place[1]] = jnp.where((row == 0) | (row == 7), roll(t, -3), zero)
            edge[f, place[2]] = zero
    for f in range(3):
        for x in range(4):
            cbody[f, 3 + x] = couple[f, x]
            cedge[f, 3 + x] = crim[f, x]
        for buf, place in ((before, (2, 1)), (after, (7, 8))):
            for d in range(2):
                cbody[f, place[d]] = buf[24 + 2 * f + d]
            cedge[f, place[0]] = jnp.where((row == 0) | (row == 7), roll(buf[38], -2 * f), zero)
            cedge[f, place[1]] = zero

    def along(b, e):
        ub, ue, db, de = roll(b, -1), roll(e, -1), roll(b, 1), roll(e, 1)
        sb = jnp.where(row == 7, ue, ub) + jnp.where(row == 0, de, db)
        se = jnp.where(row == 7, ub, ue) + jnp.where(row == 0, db, de)
        return sb + depth(b), se + depth(e)

    def depth(t):
        up = jnp.where(lane == 255, zero, pltpu.roll(t, 255, 1))
        down = jnp.where(lane == 0, zero, pltpu.roll(t, 1, 1))
        return up + down

    def diagonal(x, _):
        for f in range(4):
            b, e = body[4 + f, x], edge[4 + f, x]
            sb, se = along(b, e)
            sb = sb + (body[4 + f, x - 1] + body[4 + f, x + 1])
            se = se + (edge[4 + f, x - 1] + edge[4 + f, x + 1])
            dbody[f, x] = SHIFT[f] + b * sb
            dedge[f, x] = SHIFT[f] + e * se
        return 0

    lax.fori_loop(1, 9, diagonal, 0)

    def scale(x, _):
        for f in range(4):
            ubody[f, x] = body[f, x] * body[4 + f, x]
            uedge[f, x] = edge[f, x] * edge[4 + f, x]
        return 0

    def mix(v):
        return WEIGHT[0] * (v[0] - v[3]) + (v[1] - v[2])

    def apply(low, high, out):
        lax.fori_loop(low - 1, high + 1, scale, 0)

        def step(x, _):
            vb, ve = [body[f, x] for f in range(4)], [edge[f, x] for f in range(4)]
            mb, me = mix(vb), mix(ve)
            cb = [cbody[f, x] * mb for f in range(3)]
            ce = [cedge[f, x] * me for f in range(3)]
            cb, ce = [cb[2], -cb[0], cb[0], cb[1]], [ce[2], -ce[0], ce[0], ce[1]]
            for f in range(4):
                sb, se = along(ubody[f, x], uedge[f, x])
                sb = sb + (ubody[f, x - 1] + ubody[f, x + 1])
                se = se + (uedge[f, x - 1] + uedge[f, x + 1])
                body[f, x] = dbody[f, x] * vb[f] - body[4 + f, x] * sb + cb[f]
                edge[f, x] = dedge[f, x] * ve[f] - edge[4 + f, x] * se + ce[f]
            return 0

        lax.fori_loop(low, high, step, 0)
        for f in range(4):
            for x in range(4):
                out[f, x] = body[f, 3 + x]

    apply(1, 9, k1)
    apply(2, 8, k2)
    apply(3, 7, k3)

    def inner(x, sums):
        for f in range(4):
            v = [source[f, x], k1[f, x], k2[f, x], k3[f, x]]
            sums = [s + v[i] * v[j] for s, (i, j) in zip(sums, PAIRS)]
        return sums

    sums = lax.fori_loop(0, 4, inner, [zero] * 10)
    place = lax.broadcasted_iota(jnp.int32, (1, 128), 1)
    line = jnp.zeros((1, 128), F32)
    for index, s in enumerate(sums):
        total = jnp.sum(jnp.sum(s, axis=0, keepdims=True), axis=1, keepdims=True)
        line = jnp.where(place == index, total, line)
    gram[...] = line


def least_squares(columns, beta):
    count = len(columns)
    zero = beta * 0.0
    table = [
        [columns[col][r] if r <= col + 1 else zero for col in range(count)]
        for r in range(count + 1)
    ]
    target = [beta] + [zero] * count
    for col in range(count):
        upper, lower = table[col][col], table[col + 1][col]
        radius = jnp.sqrt(upper * upper + lower * lower)
        cosine, sine = upper / radius, lower / radius
        for other in range(col, count):
            first, second = table[col][other], table[col + 1][other]
            table[col][other] = cosine * first + sine * second
            table[col + 1][other] = -sine * first + cosine * second
        first, second = target[col], target[col + 1]
        target[col] = cosine * first + sine * second
        target[col + 1] = -sine * first + cosine * second
    solved = [zero] * count
    for r in range(count - 1, -1, -1):
        value = target[r]
        for other in range(r + 1, count):
            value = value - table[r][other] * solved[other]
        solved[r] = value / table[r][r]
    return solved


def total(terms):
    out = terms[0]
    for t in terms[1:]:
        out = out + t
    return out


def coefficients(g):
    def dot(u, v):
        return total([total([g[i][j] * v[j] for j in range(len(v))]) * u[i] for i in range(len(u))])

    beta = jnp.sqrt(g[0][0] + EPS)
    basis = [[1.0 / beta]]
    columns = []
    for k in range(3):
        z = [beta * 0.0] + basis[k]
        projections = [dot(basis[i], z) for i in range(k + 1)]
        for i in range(k + 1):
            z = [
                z[j] - projections[i] * basis[i][j] if j < len(basis[i]) else z[j]
                for j in range(k + 2)
            ]
        length = jnp.sqrt(jnp.maximum(dot(z, z), 0.0) + EPS)
        columns.append(projections + [length])
        basis.append([t / length for t in z])
    y = least_squares(columns, beta)
    iterate = [total([y[j] * basis[j][i] for j in range(3) if i < len(basis[j])]) for i in range(3)]
    image = [
        total([columns[col][r] * y[col] for col in range(3) if r <= col + 1]) for r in range(4)
    ]
    image[0] = image[0] - beta
    rest = [-total([image[j] * basis[j][i] for j in range(4) if i < len(basis[j])]) for i in range(4)]
    return iterate, rest


def finish(gram, source, k1, k2, k3, adjoint, residual):
    line = gram[0]
    for i in range(1, gram.shape[0]):
        line = line + gram[i]
    g = [[None] * 4 for _ in range(4)]
    for index, (i, j) in enumerate(PAIRS):
        g[i][j] = g[j][i] = line[:, index:index + 1]
    iterate, rest = coefficients(g)
    iterate = [jnp.broadcast_to(t, TILE) for t in iterate]
    rest = [jnp.broadcast_to(t, TILE) for t in rest]
    vectors = (source, k1, k2, k3)
    for f in range(4):
        for x in range(4):
            v = [ref[f, x] for ref in vectors]
            adjoint[f, x] = total([c * t for c, t in zip(iterate, v)])
            residual[f, x] = total([c * t for c, t in zip(rest, v)])


def call(kernel, ins, outs, scratch=()):
    return pl.pallas_call(
        kernel,
        out_shape=[jax.ShapeDtypeStruct(s, F32) for s in outs],
        in_specs=[VMEM] * ins,
        out_specs=[VMEM] * len(outs),
        scratch_shapes=[pltpu.VMEM(s, F32) for s in scratch],
        compiler_params=pltpu.CompilerParams(vmem_limit_bytes=16 * 2**20),
    )


def swap(to_right, to_left, axis):
    size = lax.axis_size(axis)
    up = [(i, i + 1) for i in range(size - 1)]
    down = [(i + 1, i) for i in range(size - 1)]
    return lax.ppermute(to_right, axis, up), lax.ppermute(to_left, axis, down)


def local(source, labels, mask, conduct, rate):
    four, three = (4, 4) + TILE, (3, 4) + TILE
    kcell, couple, to_right, to_left = call(
        prepare, 5, [four, three, (Y_TILES,) + TILE, (Y_TILES,) + TILE]
    )(source, labels, mask, conduct, rate)
    from_left, from_right = swap(to_right, to_left, "gy")
    rim, crim, to_right, to_left = call(
        widen, 5, [(8, 4) + TILE, three, (X_TILES,) + TILE, (X_TILES,) + TILE]
    )(source, kcell, couple, from_left, from_right)
    before, after = swap(to_right, to_left, "gx")
    wide = (4, 10) + TILE
    k1, k2, k3, gram = call(
        krylov,
        7,
        [four, four, four, (1, 128)],
        [(8, 10) + TILE] * 2 + [(3, 10) + TILE] * 2 + [wide] * 4,
    )(source, kcell, couple, rim, crim, before, after)
    for axis in ("gx", "gy"):
        size = lax.axis_size(axis)
        gram = lax.all_to_all(jnp.broadcast_to(gram[None], (size, 1, 128)), axis, 0, 0)
        if axis == "gx":
            gram = jnp.sum(gram, axis=0)
    return tuple(call(finish, 5, [four, four])(gram, source, k1, k2, k3))


def solution(mesh):
    return jax.shard_map(
        local,
        mesh=mesh,
        in_specs=(
            P(None, "gx", "gy", None),
            P("gx", "gy", None),
            P("gx", "gy", None),
            P(None, "gx", "gy", None),
            P(None, "gx", "gy", None),
        ),
        out_specs=(P(None, "gx", "gy", None), P(None, "gx", "gy", None)),
        check_vma=False,
    )
```

```python
import jax
import jax.numpy as jnp
from jax import lax
from jax.experimental import pallas as pl
from jax.experimental.pallas import tpu as pltpu
from jax.sharding import PartitionSpec as P

PHASE = ((1.0, 0.08, 0.08), (1.0, 0.08, 0.08), (0.08, 1.0, 1.0), (0.08, 1.0, 0.08))
SHIFT = (1.0, 0.5, 0.5, 1.0)
WEIGHT = (0.8, 1.0, -1.0, -0.8)
EPS = 1e-12
F32 = jnp.float32
VMEM = pl.BlockSpec(memory_space=pltpu.VMEM)
HBM = pl.BlockSpec(memory_space=pltpu.HBM)
TILE = (8, 256)
Y_TILES = 19
X_TILES = 39
PAIRS = [(i, j) for i in range(4) for j in range(i, 4)]


def rows():
    return lax.broadcasted_iota(jnp.int32, TILE, 0)


def roll(tile, by):
    by = by % 8
    return tile if by == 0 else pltpu.roll(tile, by, 0)


def prepare(source_in, labels_in, mask_in, conduct_in, rate_in,
            source, kcell, couple, to_right, to_left,
            labels, mask, conduct, rate, arrived):
    pairs = ((conduct_in, conduct), (labels_in, labels), (source_in, source), (rate_in, rate), (mask_in, mask))
    copies = [pltpu.make_async_copy(a, b, arrived.at[i]) for i, (a, b) in enumerate(pairs)]
    for c in copies:
        c.start()
    row = rows()

    def faces(f, ref):
        for k in range(2):
            a, b = ref[f % 4, 2 * k], ref[f % 4, 2 * k + 1]
            to_right[2 * f + k] = jnp.where(row >= 5, a, roll(b, -3))
            to_left[2 * f + k] = jnp.where(row < 3, a, roll(b, 3))

    copies[0].wait()
    copies[1].wait()
    for x in range(4):
        phase = labels[x]
        for f in range(4):
            t = PHASE[f]
            base = jnp.where(phase == 0, t[0], jnp.where(phase == 1, t[1], t[2]))
            kcell[f, x] = base * conduct[f, x].astype(F32)
    for f in range(4):
        faces(4 + f, kcell)
    copies[2].wait()
    for f in range(4):
        faces(f, source)
    copies[3].wait()
    copies[4].wait()
    for x in range(4):
        interface = mask[x].astype(F32)
        for f in range(3):
            couple[f, x] = rate[f, x].astype(F32) * interface
    for f in range(3):
        right, left = couple[f, 0], couple[f, 0]
        for x in range(1, 4):
            right = jnp.where(row >= 8 - 2 * x, right, roll(couple[f, x], -2 * x))
            left = jnp.where(row < 2 * x, left, roll(couple[f, x], 2 * x))
        to_right[16 + f] = right
        to_left[16 + f] = left


def widen(source, kcell, couple, from_left, from_right, rim, crim, to_right, to_left):
    row = rows()
    for f in range(8):
        for x in range(4):
            k, b = 2 * f + x // 2, 3 * (x % 2)
            left, right = roll(from_left[k], b), roll(from_right[k], -b)
            rim[f, x] = jnp.where(row < 4, right, left)
    for f in range(3):
        for x in range(4):
            left, right = roll(from_left[16 + f], 2 * x), roll(from_right[16 + f], -2 * x)
            crim[f, x] = jnp.where(row < 4, right, left)
    for out, order in ((to_right, (3, 2, 1)), (to_left, (0, 1, 2))):
        for f in range(8):
            ref = source if f < 4 else kcell
            for d in range(3):
                out[3 * f + d] = ref[f % 4, order[d]]
            out[30 + f] = jnp.where((row == 2) | (row == 3), roll(rim[f, order[1]], 3), rim[f, order[0]])
        for f in range(3):
            for d in range(2):
                out[24 + 2 * f + d] = couple[f, order[d]]
        c = [roll(crim[f, order[0]], 2 * f) for f in range(3)]
        out[38] = jnp.where((row == 0) | (row == 7), c[0], jnp.where(row <= 2, c[1], c[2]))


def krylov(source, kcell, couple, rim, crim, before, after, k1, k2, k3, gram,
           far, cfar, vbody, vedge, dbody, dedge, ubody, uedge):
    row = rows()
    lane = lax.broadcasted_iota(jnp.int32, TILE, 1)
    zero = jnp.zeros(TILE, F32)
    sides = {2: (before, 0), 1: (before, 1), 0: (before, 2), 7: (after, 0), 8: (after, 1), 9: (after, 2)}
    slot = {1: 0, 2: 1, 7: 2, 8: 3}
    for f in range(8):
        for x in (1, 2, 7, 8):
            buf, d = sides[x]
            far[f, slot[x]] = roll(buf[30 + f], -3 * d)
    for f in range(3):
        for buf, k in ((before, 0), (after, 1)):
            cfar[f, k] = roll(buf[38], -2 * f)

    def whole(f, x):
        if 3 <= x <= 6:
            return (source if f < 4 else kcell)[f % 4, x - 3]
        buf, d = sides[x]
        return buf[3 * f + d]

    def border(f, x):
        return rim[f, x - 3] if 3 <= x <= 6 else far[f, slot[x]]

    def couple_body(f, x):
        if 3 <= x <= 6:
            return couple[f, x - 3]
        buf, d = sides[x]
        return buf[24 + 2 * f + d]

    def couple_edge(f, x):
        return crim[f, x - 3] if 3 <= x <= 6 else cfar[f, 0 if x == 2 else 1]

    def along(t, other):
        up = roll(jnp.where(row == 0, other, t), -1)
        down = roll(jnp.where(row == 7, other, t), 1)
        ahead = jnp.where(lane == 255, zero, pltpu.roll(t, 255, 1))
        back = jnp.where(lane == 0, zero, pltpu.roll(t, 1, 1))
        return (up + down) + (ahead + back)

    def mix(v):
        return WEIGHT[0] * (v[0] - v[3]) + (v[1] - v[2])

    def interface(c, v):
        m = mix(v)
        a, b, c = c[0] * m, c[1] * m, c[2] * m
        return [c, -a, a, b]

    for x in range(10):
        for f in range(4):
            ubody[0, f, x] = whole(f, x) * whole(4 + f, x)
            if 1 <= x <= 8:
                uedge[0, f, x] = border(f, x) * border(4 + f, x)

    outs = (None, k1, k2, k3)

    def vector(level, edge, f, x):
        if level == 0:
            return border(f, x) if edge else whole(f, x)
        if edge:
            return vedge[level - 1, f, x]
        return outs[level][f, x - 3] if 3 <= x <= 6 else vbody[level - 1, f, x]

    def step(level, edge, x):
        u, other, diagonal = (uedge, ubody, dedge) if edge else (ubody, uedge, dbody)
        now, later = level % 2, (level + 1) % 2
        v = [vector(level, edge, f, x) for f in range(4)]
        c = interface([(couple_edge if edge else couple_body)(f, x) for f in range(3)], v)
        new = []
        for f in range(4):
            own = border(4 + f, x) if edge else whole(4 + f, x)
            side = border if edge else whole
            if level == 0:
                k = along(own, whole(4 + f, x) if edge else border(4 + f, x))
                k = k + (side(4 + f, x - 1) + side(4 + f, x + 1))
                d = SHIFT[f] + own * k
                diagonal[f, x] = d
            else:
                d = diagonal[f, x]
            s = along(u[now, f, x], other[now, f, x]) + (u[now, f, x - 1] + u[now, f, x + 1])
            t = d * v[f] - own * s + c[f]
            if level < 2:
                u[later, f, x] = own * t
            if edge:
                vedge[level, f, x] = t
            elif 3 <= x <= 6:
                outs[level + 1][f, x - 3] = t
            else:
                vbody[level, f, x] = t
            new.append(t)
        return new

    for level in range(2):
        for x in range(1 + level, 9 - level):
            step(level, False, x)
            if 2 + level <= x <= 7 - level:
                step(level, True, x)
    sums = [zero] * 10
    for x in range(3, 7):
        last = step(2, False, x)
        for f in range(4):
            v = [source[f, x - 3], k1[f, x - 3], k2[f, x - 3], last[f]]
            sums = [s + v[i] * v[j] for s, (i, j) in zip(sums, PAIRS)]
    place = lax.broadcasted_iota(jnp.int32, (1, 128), 1)
    line = jnp.zeros((1, 128), F32)
    for index, s in enumerate(sums):
        whole_sum = jnp.sum(jnp.sum(s, axis=0, keepdims=True), axis=1, keepdims=True)
        line = jnp.where(place == index, whole_sum, line)
    gram[...] = line


def least_squares(columns, beta):
    count = len(columns)
    zero = beta * 0.0
    table = [
        [columns[col][r] if r <= col + 1 else zero for col in range(count)]
        for r in range(count + 1)
    ]
    target = [beta] + [zero] * count
    for col in range(count):
        upper, lower = table[col][col], table[col + 1][col]
        radius = jnp.sqrt(upper * upper + lower * lower)
        cosine, sine = upper / radius, lower / radius
        for other in range(col, count):
            first, second = table[col][other], table[col + 1][other]
            table[col][other] = cosine * first + sine * second
            table[col + 1][other] = -sine * first + cosine * second
        first, second = target[col], target[col + 1]
        target[col] = cosine * first + sine * second
        target[col + 1] = -sine * first + cosine * second
    solved = [zero] * count
    for r in range(count - 1, -1, -1):
        value = target[r]
        for other in range(r + 1, count):
            value = value - table[r][other] * solved[other]
        solved[r] = value / table[r][r]
    return solved


def total(terms):
    out = terms[0]
    for t in terms[1:]:
        out = out + t
    return out


def coefficients(g):
    def dot(u, v):
        return total([total([g[i][j] * v[j] for j in range(len(v))]) * u[i] for i in range(len(u))])

    beta = jnp.sqrt(g[0][0] + EPS)
    basis = [[1.0 / beta]]
    columns = []
    for k in range(3):
        z = [beta * 0.0] + basis[k]
        projections = [dot(basis[i], z) for i in range(k + 1)]
        for i in range(k + 1):
            z = [
                z[j] - projections[i] * basis[i][j] if j < len(basis[i]) else z[j]
                for j in range(k + 2)
            ]
        length = jnp.sqrt(jnp.maximum(dot(z, z), 0.0) + EPS)
        columns.append(projections + [length])
        basis.append([t / length for t in z])
    y = least_squares(columns, beta)
    iterate = [total([y[j] * basis[j][i] for j in range(3) if i < len(basis[j])]) for i in range(3)]
    image = [
        total([columns[col][r] * y[col] for col in range(3) if r <= col + 1]) for r in range(4)
    ]
    image[0] = image[0] - beta
    rest = [-total([image[j] * basis[j][i] for j in range(4) if i < len(basis[j])]) for i in range(4)]
    return iterate, rest


def finish(gram, source, k1, k2, k3, adjoint_out, residual_out, adjoint, residual, left):
    line = gram[0]
    for i in range(1, gram.shape[0]):
        line = line + gram[i]
    g = [[None] * 4 for _ in range(4)]
    for index, (i, j) in enumerate(PAIRS):
        g[i][j] = g[j][i] = line[:, index:index + 1]
    iterate, rest = coefficients(g)
    iterate = [jnp.broadcast_to(t, TILE) for t in iterate]
    rest = [jnp.broadcast_to(t, TILE) for t in rest]
    vectors = (source, k1, k2, k3)
    copies = []
    for f in range(4):
        for x in range(4):
            v = [ref[f, x] for ref in vectors]
            adjoint[f, x] = total([c * t for c, t in zip(iterate, v)])
            residual[f, x] = total([c * t for c, t in zip(rest, v)])
        copies.append(pltpu.make_async_copy(adjoint.at[f], adjoint_out.at[f], left.at[2 * f]))
        copies.append(pltpu.make_async_copy(residual.at[f], residual_out.at[f], left.at[2 * f + 1]))
        for c in copies[-2:]:
            c.start()
    for c in copies:
        c.wait()


def call(kernel, ins, outs, scratch=(), spaces=(VMEM, VMEM)):
    return pl.pallas_call(
        kernel,
        out_shape=[jax.ShapeDtypeStruct(s, F32) for s in outs],
        in_specs=[spaces[0]] * ins,
        out_specs=[spaces[1]] * len(outs),
        scratch_shapes=[s if not isinstance(s, tuple) else pltpu.VMEM(s, F32) for s in scratch],
        compiler_params=pltpu.CompilerParams(vmem_limit_bytes=16 * 2**20),
    )


def swap(to_right, to_left, axis):
    size = lax.axis_size(axis)
    up = [(i, i + 1) for i in range(size - 1)]
    down = [(i + 1, i) for i in range(size - 1)]
    return lax.ppermute(to_right, axis, up), lax.ppermute(to_left, axis, down)


def run_krylov(*args):
    four, wide = (4, 4) + TILE, (4, 10) + TILE
    return call(
        krylov,
        7,
        [four, four, four, (1, 128)],
        [(8, 4) + TILE, (3, 2) + TILE] + [(2, 4, 10) + TILE] * 2 + [wide] * 2 + [(2, 4, 10) + TILE] * 2,
    )(*args)


def run_finish(*args):
    four = (4, 4) + TILE
    own = [four, four, pltpu.SemaphoreType.DMA((8,))]
    return tuple(call(finish, 5, [four, four], own, (VMEM, HBM))(*args))


def local(source, labels, mask, conduct, rate):
    four, three = (4, 4) + TILE, (3, 4) + TILE
    source, kcell, couple, to_right, to_left = call(
        prepare,
        5,
        [four, four, three, (Y_TILES,) + TILE, (Y_TILES,) + TILE],
        [
            pltpu.VMEM((4,) + TILE, jnp.int32),
            pltpu.VMEM((4,) + TILE, jnp.int32),
            pltpu.VMEM(four, jnp.bfloat16),
            pltpu.VMEM(three, jnp.bfloat16),
            pltpu.SemaphoreType.DMA((5,)),
        ],
        (HBM, VMEM),
    )(*[pltpu.with_memory_space_constraint(t, pltpu.HBM) for t in (source, labels, mask, conduct, rate)])
    from_left, from_right = swap(to_right, to_left, "gy")
    rim, crim, to_right, to_left = call(
        widen, 5, [(8, 4) + TILE, three, (X_TILES,) + TILE, (X_TILES,) + TILE]
    )(source, kcell, couple, from_left, from_right)
    before, after = swap(to_right, to_left, "gx")
    k1, k2, k3, gram = run_krylov(source, kcell, couple, rim, crim, before, after)
    for axis in ("gx", "gy"):
        size = lax.axis_size(axis)
        gram = lax.all_to_all(jnp.broadcast_to(gram[None], (size, 1, 128)), axis, 0, 0)
        if axis == "gx":
            gram = jnp.sum(gram, axis=0)
    return run_finish(gram, source, k1, k2, k3)


def solution(mesh):
    return jax.shard_map(
        local,
        mesh=mesh,
        in_specs=(
            P(None, "gx", "gy", None),
            P("gx", "gy", None),
            P("gx", "gy", None),
            P(None, "gx", "gy", None),
            P(None, "gx", "gy", None),
        ),
        out_specs=(P(None, "gx", "gy", None), P(None, "gx", "gy", None)),
        check_vma=False,
    )
```

```python
import jax
import jax.numpy as jnp
from jax import lax
from jax.experimental import pallas as pl
from jax.experimental.pallas import tpu as pltpu
from jax.sharding import PartitionSpec as P

PHASE = ((1.0, 0.08, 0.08), (1.0, 0.08, 0.08), (0.08, 1.0, 1.0), (0.08, 1.0, 0.08))
SHIFT = (1.0, 0.5, 0.5, 1.0)
WEIGHT = (0.8, 1.0, -1.0, -0.8)
EPS = 1e-12
F32 = jnp.float32
VMEM = pl.BlockSpec(memory_space=pltpu.VMEM)
HBM = pl.BlockSpec(memory_space=pltpu.HBM)
TILE = (8, 256)
Y_TILES = 19
X_TILES = 30
CORNER_TILES = 9
PAIRS = [(i, j) for i in range(4) for j in range(i, 4)]


def rows():
    return lax.broadcasted_iota(jnp.int32, TILE, 0)


def roll(tile, by):
    by = by % 8
    return tile if by == 0 else pltpu.roll(tile, by, 0)


def prepare(source_in, labels_in, mask_in, conduct_in, rate_in,
            source, kcell, couple, to_right, to_left,
            labels, mask, conduct, rate, arrived):
    pairs = ((conduct_in, conduct), (labels_in, labels), (source_in, source), (rate_in, rate), (mask_in, mask))
    copies = [pltpu.make_async_copy(a, b, arrived.at[i]) for i, (a, b) in enumerate(pairs)]
    for c in copies:
        c.start()
    row = rows()

    def faces(f, ref):
        for k in range(2):
            a, b = ref[f % 4, 2 * k], ref[f % 4, 2 * k + 1]
            to_right[2 * f + k] = jnp.where(row >= 5, a, roll(b, -3))
            to_left[2 * f + k] = jnp.where(row < 3, a, roll(b, 3))

    copies[0].wait()
    copies[1].wait()
    for x in range(4):
        phase = labels[x]
        for f in range(4):
            t = PHASE[f]
            base = jnp.where(phase == 0, t[0], jnp.where(phase == 1, t[1], t[2]))
            kcell[f, x] = base * conduct[f, x].astype(F32)
    for f in range(4):
        faces(4 + f, kcell)
    copies[2].wait()
    for f in range(4):
        faces(f, source)
    copies[3].wait()
    copies[4].wait()
    for x in range(4):
        interface = mask[x].astype(F32)
        for f in range(3):
            couple[f, x] = rate[f, x].astype(F32) * interface
    for f in range(3):
        right, left = couple[f, 0], couple[f, 0]
        for x in range(1, 4):
            right = jnp.where(row >= 8 - 2 * x, right, roll(couple[f, x], -2 * x))
            left = jnp.where(row < 2 * x, left, roll(couple[f, x], 2 * x))
        to_right[16 + f] = right
        to_left[16 + f] = left


def columns_beside(source, kcell, couple, to_next, to_last):
    for out, order in ((to_next, (3, 2, 1)), (to_last, (0, 1, 2))):
        for d in range(3):
            for f in range(8):
                out[3 * f + d] = (source if f < 4 else kcell)[f % 4, order[d]]
            for f in range(3 if d < 2 else 0):
                out[24 + 2 * f + d] = couple[f, order[d]]


def widen(from_left, from_right, rim, crim, to_next, to_last):
    row = rows()
    for f in range(8):
        for x in range(4):
            k, b = 2 * f + x // 2, 3 * (x % 2)
            left, right = roll(from_left[k], b), roll(from_right[k], -b)
            rim[f, x] = jnp.where(row < 4, right, left)
    for f in range(3):
        for x in range(4):
            left, right = roll(from_left[16 + f], 2 * x), roll(from_right[16 + f], -2 * x)
            crim[f, x] = jnp.where(row < 4, right, left)
    for out, order in ((to_next, (3, 2)), (to_last, (0, 1))):
        for f in range(8):
            out[f] = jnp.where((row == 2) | (row == 3), roll(rim[f, order[1]], 3), rim[f, order[0]])
        c = [roll(crim[f, order[0]], 2 * f) for f in range(3)]
        out[8] = jnp.where((row == 0) | (row == 7), c[0], jnp.where(row <= 2, c[1], c[2]))


def krylov(source, kcell, couple, rim, crim, before, after, corner_before, corner_after,
           k1, k2, k3, gram,
           far, cfar, vbody, vedge, dbody, dedge, ubody, uedge):
    row = rows()
    lane = lax.broadcasted_iota(jnp.int32, TILE, 1)
    zero = jnp.zeros(TILE, F32)
    sides = {2: (before, 0), 1: (before, 1), 0: (before, 2), 7: (after, 0), 8: (after, 1), 9: (after, 2)}
    slot = {1: 0, 2: 1, 7: 2, 8: 3}
    for f in range(8):
        for x in (1, 2, 7, 8):
            corner = corner_before if x < 3 else corner_after
            far[f, slot[x]] = roll(corner[f], -3 * sides[x][1])
    for f in range(3):
        for corner, k in ((corner_before, 0), (corner_after, 1)):
            cfar[f, k] = roll(corner[8], -2 * f)

    def whole(f, x):
        if 3 <= x <= 6:
            return (source if f < 4 else kcell)[f % 4, x - 3]
        buf, d = sides[x]
        return buf[3 * f + d]

    def border(f, x):
        return rim[f, x - 3] if 3 <= x <= 6 else far[f, slot[x]]

    def couple_body(f, x):
        if 3 <= x <= 6:
            return couple[f, x - 3]
        buf, d = sides[x]
        return buf[24 + 2 * f + d]

    def couple_edge(f, x):
        return crim[f, x - 3] if 3 <= x <= 6 else cfar[f, 0 if x == 2 else 1]

    def along(t, other):
        up = roll(jnp.where(row == 0, other, t), -1)
        down = roll(jnp.where(row == 7, other, t), 1)
        ahead = jnp.where(lane == 255, zero, pltpu.roll(t, 255, 1))
        back = jnp.where(lane == 0, zero, pltpu.roll(t, 1, 1))
        return (up + down) + (ahead + back)

    def mix(v):
        return WEIGHT[0] * (v[0] - v[3]) + (v[1] - v[2])

    def interface(c, v):
        m = mix(v)
        a, b, c = c[0] * m, c[1] * m, c[2] * m
        return [c, -a, a, b]

    for x in range(10):
        for f in range(4):
            ubody[0, f, x] = whole(f, x) * whole(4 + f, x)
            if 1 <= x <= 8:
                uedge[0, f, x] = border(f, x) * border(4 + f, x)

    outs = (None, k1, k2, k3)

    def vector(level, edge, f, x):
        if level == 0:
            return border(f, x) if edge else whole(f, x)
        if edge:
            return vedge[level - 1, f, x]
        return outs[level][f, x - 3] if 3 <= x <= 6 else vbody[level - 1, f, x]

    def step(level, edge, x):
        u, other, diagonal = (uedge, ubody, dedge) if edge else (ubody, uedge, dbody)
        now, later = level % 2, (level + 1) % 2
        v = [vector(level, edge, f, x) for f in range(4)]
        c = interface([(couple_edge if edge else couple_body)(f, x) for f in range(3)], v)
        new = []
        for f in range(4):
            own = border(4 + f, x) if edge else whole(4 + f, x)
            side = border if edge else whole
            if level == 0:
                k = along(own, whole(4 + f, x) if edge else border(4 + f, x))
                k = k + (side(4 + f, x - 1) + side(4 + f, x + 1))
                d = SHIFT[f] + own * k
                diagonal[f, x] = d
            else:
                d = diagonal[f, x]
            s = along(u[now, f, x], other[now, f, x]) + (u[now, f, x - 1] + u[now, f, x + 1])
            t = d * v[f] - own * s + c[f]
            if level < 2:
                u[later, f, x] = own * t
            if edge:
                vedge[level, f, x] = t
            elif 3 <= x <= 6:
                outs[level + 1][f, x - 3] = t
            else:
                vbody[level, f, x] = t
            new.append(t)
        return new

    for level in range(2):
        for x in range(1 + level, 9 - level):
            step(level, False, x)
            if 2 + level <= x <= 7 - level:
                step(level, True, x)
    sums = [zero] * 10
    for x in range(3, 7):
        last = step(2, False, x)
        for f in range(4):
            v = [source[f, x - 3], k1[f, x - 3], k2[f, x - 3], last[f]]
            sums = [s + v[i] * v[j] for s, (i, j) in zip(sums, PAIRS)]
    place = lax.broadcasted_iota(jnp.int32, (1, 128), 1)
    line = jnp.zeros((1, 128), F32)
    for index, s in enumerate(sums):
        whole_sum = jnp.sum(jnp.sum(s, axis=0, keepdims=True), axis=1, keepdims=True)
        line = jnp.where(place == index, whole_sum, line)
    gram[...] = line


def least_squares(columns, beta):
    count = len(columns)
    zero = beta * 0.0
    table = [
        [columns[col][r] if r <= col + 1 else zero for col in range(count)]
        for r in range(count + 1)
    ]
    target = [beta] + [zero] * count
    scales = []
    for col in range(count):
        upper, lower = table[col][col], table[col + 1][col]
        scale = lax.rsqrt(upper * upper + lower * lower)
        cosine, sine = upper * scale, lower * scale
        scales.append(scale)
        for other in range(col + 1, count):
            first, second = table[col][other], table[col + 1][other]
            table[col][other] = cosine * first + sine * second
            table[col + 1][other] = -sine * first + cosine * second
        first, second = target[col], target[col + 1]
        target[col] = cosine * first + sine * second
        target[col + 1] = -sine * first + cosine * second
    solved = [zero] * count
    for r in range(count - 1, -1, -1):
        value = target[r]
        for other in range(r + 1, count):
            value = value - table[r][other] * solved[other]
        solved[r] = value * scales[r]
    return solved


def total(terms):
    out = terms[0]
    for t in terms[1:]:
        out = out + t
    return out


def coefficients(g):
    def dot(u, v):
        return total([total([g[i][j] * v[j] for j in range(len(v))]) * u[i] for i in range(len(u))])

    square = g[0][0] + EPS
    inverse = lax.rsqrt(square)
    beta = square * inverse
    basis = [[inverse]]
    columns = []
    for k in range(3):
        z = [beta * 0.0] + basis[k]
        projections = [dot(basis[i], z) for i in range(k + 1)]
        for i in range(k + 1):
            z = [
                z[j] - projections[i] * basis[i][j] if j < len(basis[i]) else z[j]
                for j in range(k + 2)
            ]
        square = jnp.maximum(dot(z, z), 0.0) + EPS
        inverse = lax.rsqrt(square)
        columns.append(projections + [square * inverse])
        basis.append([t * inverse for t in z])
    y = least_squares(columns, beta)
    iterate = [total([y[j] * basis[j][i] for j in range(3) if i < len(basis[j])]) for i in range(3)]
    image = [
        total([columns[col][r] * y[col] for col in range(3) if r <= col + 1]) for r in range(4)
    ]
    image[0] = image[0] - beta
    rest = [-total([image[j] * basis[j][i] for j in range(4) if i < len(basis[j])]) for i in range(4)]
    return iterate, rest


def finish(gram, source, k1, k2, k3, adjoint_out, residual_out, adjoint, residual, left):
    line = gram[0]
    for i in range(1, gram.shape[0]):
        line = line + gram[i]
    g = [[None] * 4 for _ in range(4)]
    for index, (i, j) in enumerate(PAIRS):
        g[i][j] = g[j][i] = line[:, index:index + 1]
    iterate, rest = coefficients(g)
    iterate = [jnp.broadcast_to(t, TILE) for t in iterate]
    rest = [jnp.broadcast_to(t, TILE) for t in rest]
    vectors = (source, k1, k2, k3)
    copies = []
    for f in range(4):
        for x in range(4):
            v = [ref[f, x] for ref in vectors]
            adjoint[f, x] = total([c * t for c, t in zip(iterate, v)])
            residual[f, x] = total([c * t for c, t in zip(rest, v)])
        copies.append(pltpu.make_async_copy(adjoint.at[f], adjoint_out.at[f], left.at[2 * f]))
        copies.append(pltpu.make_async_copy(residual.at[f], residual_out.at[f], left.at[2 * f + 1]))
        for c in copies[-2:]:
            c.start()
    for c in copies:
        c.wait()


def call(kernel, ins, outs, scratch=(), spaces=(VMEM, VMEM), cost=None):
    return pl.pallas_call(
        kernel,
        out_shape=[jax.ShapeDtypeStruct(s, F32) for s in outs],
        in_specs=[spaces[0]] * ins,
        out_specs=[spaces[1]] * len(outs),
        scratch_shapes=[s if not isinstance(s, tuple) else pltpu.VMEM(s, F32) for s in scratch],
        cost_estimate=cost,
        compiler_params=pltpu.CompilerParams(vmem_limit_bytes=16 * 2**20),
    )


def swap(to_right, to_left, axis):
    size = lax.axis_size(axis)
    up = [(i, i + 1) for i in range(size - 1)]
    down = [(i + 1, i) for i in range(size - 1)]
    return lax.ppermute(to_right, axis, up), lax.ppermute(to_left, axis, down)


def run_krylov(*args):
    four, wide = (4, 4) + TILE, (4, 10) + TILE
    return call(
        krylov,
        9,
        [four, four, four, (1, 128)],
        [(8, 4) + TILE, (3, 2) + TILE] + [(2, 4, 10) + TILE] * 2 + [wide] * 2 + [(2, 4, 10) + TILE] * 2,
    )(*args)


def run_finish(*args):
    four = (4, 4) + TILE
    own = [four, four, pltpu.SemaphoreType.DMA((8,))]
    return tuple(call(finish, 5, [four, four], own, (VMEM, HBM))(*args))


def local(source, labels, mask, conduct, rate):
    four, three = (4, 4) + TILE, (3, 4) + TILE
    source, kcell, couple, to_right, to_left = call(
        prepare,
        5,
        [four, four, three] + [(Y_TILES,) + TILE] * 2,
        [
            pltpu.VMEM((4,) + TILE, jnp.int32),
            pltpu.VMEM((4,) + TILE, jnp.int32),
            pltpu.VMEM(four, jnp.bfloat16),
            pltpu.VMEM(three, jnp.bfloat16),
            pltpu.SemaphoreType.DMA((5,)),
        ],
        (HBM, VMEM),
    )(*[pltpu.with_memory_space_constraint(t, pltpu.HBM) for t in (source, labels, mask, conduct, rate)])
    from_left, from_right = swap(to_right, to_left, "gy")
    to_next, to_last = call(
        columns_beside, 3, [(X_TILES,) + TILE] * 2,
        cost=pl.CostEstimate(flops=0, bytes_accessed=10**3, transcendentals=0),
    )(source, kcell, couple)
    before, after = swap(to_next, to_last, "gx")
    rim, crim, to_next, to_last = call(
        widen, 2, [(8, 4) + TILE, three] + [(CORNER_TILES,) + TILE] * 2,
        cost=pl.CostEstimate(flops=1000000000, bytes_accessed=10**3, transcendentals=0),
    )(from_left, from_right)
    corner_before, corner_after = swap(to_next, to_last, "gx")
    k1, k2, k3, gram = run_krylov(
        source, kcell, couple, rim, crim, before, after, corner_before, corner_after
    )
    for axis in ("gx", "gy"):
        size = lax.axis_size(axis)
        gram = lax.all_to_all(jnp.broadcast_to(gram[None], (size, 1, 128)), axis, 0, 0)
        if axis == "gx":
            gram = jnp.sum(gram, axis=0)
    return run_finish(gram, source, k1, k2, k3)


def solution(mesh):
    return jax.shard_map(
        local,
        mesh=mesh,
        in_specs=(
            P(None, "gx", "gy", None),
            P("gx", "gy", None),
            P("gx", "gy", None),
            P(None, "gx", "gy", None),
            P(None, "gx", "gy", None),
        ),
        out_specs=(P(None, "gx", "gy", None), P(None, "gx", "gy", None)),
        check_vma=False,
    )
```

```python
import jax
import jax.numpy as jnp
from jax import lax
from jax.experimental import pallas as pl
from jax.experimental.pallas import tpu as pltpu
from jax.sharding import PartitionSpec as P

PHASE = ((1.0, 0.08, 0.08), (1.0, 0.08, 0.08), (0.08, 1.0, 1.0), (0.08, 1.0, 0.08))
SHIFT = (1.0, 0.5, 0.5, 1.0)
WEIGHT = (0.8, 1.0, -1.0, -0.8)
EPS = 1e-12
F32 = jnp.float32
VMEM = pl.BlockSpec(memory_space=pltpu.VMEM)
HBM = pl.BlockSpec(memory_space=pltpu.HBM)
TILE = (8, 256)
Y_TILES = 19
X_TILES = 30
CORNER_TILES = 9
PAIRS = [(i, j) for i in range(4) for j in range(i, 4)]


def rows():
    return lax.broadcasted_iota(jnp.int32, TILE, 0)


def roll(tile, by):
    by = by % 8
    return tile if by == 0 else pltpu.roll(tile, by, 0)


def prepare(source_in, labels_in, mask_in, conduct_in, rate_in,
            source, kcell, couple, to_right, to_left,
            labels, mask, conduct, rate, arrived):
    pairs = ((conduct_in, conduct), (labels_in, labels), (source_in, source), (rate_in, rate), (mask_in, mask))
    copies = [pltpu.make_async_copy(a, b, arrived.at[i]) for i, (a, b) in enumerate(pairs)]
    for c in copies:
        c.start()
    row = rows()

    def faces(f, ref):
        for k in range(2):
            a, b = ref[f % 4, 2 * k], ref[f % 4, 2 * k + 1]
            to_right[2 * f + k] = jnp.where(row >= 5, a, roll(b, -3))
            to_left[2 * f + k] = jnp.where(row < 3, a, roll(b, 3))

    copies[0].wait()
    copies[1].wait()
    for x in range(4):
        phase = labels[x]
        for f in range(4):
            t = PHASE[f]
            base = jnp.where(phase == 0, t[0], jnp.where(phase == 1, t[1], t[2]))
            kcell[f, x] = base * conduct[f, x].astype(F32)
    for f in range(4):
        faces(4 + f, kcell)
    copies[2].wait()
    for f in range(4):
        faces(f, source)
    copies[3].wait()
    copies[4].wait()
    for x in range(4):
        interface = mask[x].astype(F32)
        for f in range(3):
            couple[f, x] = rate[f, x].astype(F32) * interface
    for f in range(3):
        right, left = couple[f, 0], couple[f, 0]
        for x in range(1, 4):
            right = jnp.where(row >= 8 - 2 * x, right, roll(couple[f, x], -2 * x))
            left = jnp.where(row < 2 * x, left, roll(couple[f, x], 2 * x))
        to_right[16 + f] = right
        to_left[16 + f] = left


def columns_from_partner():
    odd = lax.axis_index("gx") % 2
    return [k + (1 - odd) * (3 - 2 * k) for k in range(4)]


def columns_beside(source, kcell, couple, to_partner, to_other):
    own = columns_from_partner()
    for out, order in ((to_partner, own[:3]), (to_other, own[:0:-1])):
        for d in range(3):
            for f in range(8):
                out[3 * f + d] = (source if f < 4 else kcell)[f % 4, order[d]]
            for f in range(3 if d < 2 else 0):
                out[24 + 2 * f + d] = couple[f, order[d]]


def widen(from_left, from_right, rim, crim, to_partner, to_other):
    row = rows()
    for f in range(8):
        for x in range(4):
            k, b = 2 * f + x // 2, 3 * (x % 2)
            left, right = roll(from_left[k], b), roll(from_right[k], -b)
            rim[f, x] = jnp.where(row < 4, right, left)
    for f in range(3):
        for x in range(4):
            left, right = roll(from_left[16 + f], 2 * x), roll(from_right[16 + f], -2 * x)
            crim[f, x] = jnp.where(row < 4, right, left)
    own = columns_from_partner()
    for out, order in ((to_partner, own[:2]), (to_other, own[:1:-1])):
        for f in range(8):
            out[f] = jnp.where((row == 2) | (row == 3), roll(rim[f, order[1]], 3), rim[f, order[0]])
        c = [roll(crim[f, order[0]], 2 * f) for f in range(3)]
        out[8] = jnp.where((row == 0) | (row == 7), c[0], jnp.where(row <= 2, c[1], c[2]))


def krylov(source, kcell, couple, rim, crim, far, near, far_corner, near_corner,
           k1, k2, k3, gram,
           border_x, border_c, vbody, vedge, dbody, dedge, ubody, uedge):
    row = rows()
    lane = lax.broadcasted_iota(jnp.int32, TILE, 1)
    zero = jnp.zeros(TILE, F32)
    own = columns_from_partner()
    sides = {2: (near, 0), 1: (near, 1), 0: (near, 2), 7: (far, 0), 8: (far, 1), 9: (far, 2)}
    slot = {1: 0, 2: 1, 7: 2, 8: 3}
    for f in range(8):
        for x in (1, 2, 7, 8):
            corner = near_corner if x < 3 else far_corner
            border_x[f, slot[x]] = roll(corner[f], -3 * sides[x][1])
    for f in range(3):
        for corner, k in ((near_corner, 0), (far_corner, 1)):
            border_c[f, k] = roll(corner[8], -2 * f)

    def whole(f, x):
        if 3 <= x <= 6:
            return (source if f < 4 else kcell)[f % 4, own[x - 3]]
        buf, d = sides[x]
        return buf[3 * f + d]

    def border(f, x):
        return rim[f, own[x - 3]] if 3 <= x <= 6 else border_x[f, slot[x]]

    def couple_body(f, x):
        if 3 <= x <= 6:
            return couple[f, own[x - 3]]
        buf, d = sides[x]
        return buf[24 + 2 * f + d]

    def couple_edge(f, x):
        return crim[f, own[x - 3]] if 3 <= x <= 6 else border_c[f, 0 if x == 2 else 1]

    def along(t, other):
        up = roll(jnp.where(row == 0, other, t), -1)
        down = roll(jnp.where(row == 7, other, t), 1)
        ahead = jnp.where(lane == 255, zero, pltpu.roll(t, 255, 1))
        back = jnp.where(lane == 0, zero, pltpu.roll(t, 1, 1))
        return (up + down) + (ahead + back)

    def mix(v):
        return WEIGHT[0] * (v[0] - v[3]) + (v[1] - v[2])

    def interface(c, v):
        m = mix(v)
        a, b, c = c[0] * m, c[1] * m, c[2] * m
        return [c, -a, a, b]

    for x in range(10):
        for f in range(4):
            ubody[0, f, x] = whole(f, x) * whole(4 + f, x)
            if 1 <= x <= 8:
                uedge[0, f, x] = border(f, x) * border(4 + f, x)

    outs = (None, k1, k2, k3)

    def vector(level, edge, f, x):
        if level == 0:
            return border(f, x) if edge else whole(f, x)
        if edge:
            return vedge[level - 1, f, x]
        return outs[level][f, own[x - 3]] if 3 <= x <= 6 else vbody[level - 1, f, x]

    def step(level, edge, x):
        u, other, diagonal = (uedge, ubody, dedge) if edge else (ubody, uedge, dbody)
        now, later = level % 2, (level + 1) % 2
        v = [vector(level, edge, f, x) for f in range(4)]
        c = interface([(couple_edge if edge else couple_body)(f, x) for f in range(3)], v)
        new = []
        for f in range(4):
            here = border(4 + f, x) if edge else whole(4 + f, x)
            side = border if edge else whole
            if level == 0:
                k = along(here, whole(4 + f, x) if edge else border(4 + f, x))
                k = k + (side(4 + f, x - 1) + side(4 + f, x + 1))
                d = SHIFT[f] + here * k
                diagonal[f, x] = d
            else:
                d = diagonal[f, x]
            s = along(u[now, f, x], other[now, f, x]) + (u[now, f, x - 1] + u[now, f, x + 1])
            t = d * v[f] - here * s + c[f]
            if level < 2:
                u[later, f, x] = here * t
            if edge:
                vedge[level, f, x] = t
            elif 3 <= x <= 6:
                outs[level + 1][f, own[x - 3]] = t
            else:
                vbody[level, f, x] = t
            new.append(t)
        return new

    for level in range(2):
        for x in range(1 + level, 9 - level):
            step(level, False, x)
            if 2 + level <= x <= 7 - level:
                step(level, True, x)
    sums = [zero] * 10
    for x in range(3, 7):
        last = step(2, False, x)
        for f in range(4):
            v = [source[f, own[x - 3]], k1[f, own[x - 3]], k2[f, own[x - 3]], last[f]]
            sums = [s + v[i] * v[j] for s, (i, j) in zip(sums, PAIRS)]
    place = lax.broadcasted_iota(jnp.int32, (1, 128), 1)
    line = jnp.zeros((1, 128), F32)
    for index, s in enumerate(sums):
        whole_sum = jnp.sum(jnp.sum(s, axis=0, keepdims=True), axis=1, keepdims=True)
        line = jnp.where(place == index, whole_sum, line)
    gram[...] = line


def least_squares(columns, beta):
    count = len(columns)
    zero = beta * 0.0
    table = [
        [columns[col][r] if r <= col + 1 else zero for col in range(count)]
        for r in range(count + 1)
    ]
    target = [beta] + [zero] * count
    scales = []
    for col in range(count):
        upper, lower = table[col][col], table[col + 1][col]
        scale = lax.rsqrt(upper * upper + lower * lower)
        cosine, sine = upper * scale, lower * scale
        scales.append(scale)
        for other in range(col + 1, count):
            first, second = table[col][other], table[col + 1][other]
            table[col][other] = cosine * first + sine * second
            table[col + 1][other] = -sine * first + cosine * second
        first, second = target[col], target[col + 1]
        target[col] = cosine * first + sine * second
        target[col + 1] = -sine * first + cosine * second
    solved = [zero] * count
    for r in range(count - 1, -1, -1):
        value = target[r]
        for other in range(r + 1, count):
            value = value - table[r][other] * solved[other]
        solved[r] = value * scales[r]
    return solved


def total(terms):
    out = terms[0]
    for t in terms[1:]:
        out = out + t
    return out


def coefficients(g):
    def dot(u, v):
        return total([total([g[i][j] * v[j] for j in range(len(v))]) * u[i] for i in range(len(u))])

    square = g[0][0] + EPS
    inverse = lax.rsqrt(square)
    beta = square * inverse
    basis = [[inverse]]
    columns = []
    for k in range(3):
        z = [beta * 0.0] + basis[k]
        projections = [dot(basis[i], z) for i in range(k + 1)]
        for i in range(k + 1):
            z = [
                z[j] - projections[i] * basis[i][j] if j < len(basis[i]) else z[j]
                for j in range(k + 2)
            ]
        square = jnp.maximum(dot(z, z), 0.0) + EPS
        inverse = lax.rsqrt(square)
        columns.append(projections + [square * inverse])
        basis.append([t * inverse for t in z])
    y = least_squares(columns, beta)
    iterate = [total([y[j] * basis[j][i] for j in range(3) if i < len(basis[j])]) for i in range(3)]
    image = [
        total([columns[col][r] * y[col] for col in range(3) if r <= col + 1]) for r in range(4)
    ]
    image[0] = image[0] - beta
    rest = [-total([image[j] * basis[j][i] for j in range(4) if i < len(basis[j])]) for i in range(4)]
    return iterate, rest


def finish(gram, source, k1, k2, k3, adjoint_out, residual_out, adjoint, residual, left):
    line = gram[0]
    for i in range(1, gram.shape[0]):
        line = line + gram[i]
    g = [[None] * 4 for _ in range(4)]
    for index, (i, j) in enumerate(PAIRS):
        g[i][j] = g[j][i] = line[:, index:index + 1]
    iterate, rest = coefficients(g)
    iterate = [jnp.broadcast_to(t, TILE) for t in iterate]
    rest = [jnp.broadcast_to(t, TILE) for t in rest]
    vectors = (source, k1, k2, k3)
    copies = []
    for f in range(4):
        for x in range(4):
            v = [ref[f, x] for ref in vectors]
            adjoint[f, x] = total([c * t for c, t in zip(iterate, v)])
            residual[f, x] = total([c * t for c, t in zip(rest, v)])
        copies.append(pltpu.make_async_copy(adjoint.at[f], adjoint_out.at[f], left.at[2 * f]))
        copies.append(pltpu.make_async_copy(residual.at[f], residual_out.at[f], left.at[2 * f + 1]))
        for c in copies[-2:]:
            c.start()
    for c in copies:
        c.wait()


def call(kernel, ins, outs, scratch=(), spaces=(VMEM, VMEM), cost=None):
    return pl.pallas_call(
        kernel,
        out_shape=[jax.ShapeDtypeStruct(s, F32) for s in outs],
        in_specs=[spaces[0]] * ins,
        out_specs=[spaces[1]] * len(outs),
        scratch_shapes=[s if not isinstance(s, tuple) else pltpu.VMEM(s, F32) for s in scratch],
        cost_estimate=cost,
        compiler_params=pltpu.CompilerParams(vmem_limit_bytes=16 * 2**20),
    )


def swap(to_right, to_left, axis):
    size = lax.axis_size(axis)
    up = [(i, i + 1) for i in range(size - 1)]
    down = [(i + 1, i) for i in range(size - 1)]
    return lax.ppermute(to_right, axis, up), lax.ppermute(to_left, axis, down)


def exchange(to_partner, to_other):
    size = lax.axis_size("gx")
    chip = [(i, i ^ 1) for i in range(size)]
    across = [(i, ((i + 1) ^ 1) - 1) for i in range(1, size - 1)]
    return lax.ppermute(to_other, "gx", across), lax.ppermute(to_partner, "gx", chip)


def run_krylov(*args):
    four, wide = (4, 4) + TILE, (4, 10) + TILE
    return call(
        krylov,
        9,
        [four, four, four, (1, 128)],
        [(8, 4) + TILE, (3, 2) + TILE] + [(2, 4, 10) + TILE] * 2 + [wide] * 2 + [(2, 4, 10) + TILE] * 2,
    )(*args)


def run_finish(*args):
    four = (4, 4) + TILE
    own = [four, four, pltpu.SemaphoreType.DMA((8,))]
    return tuple(call(finish, 5, [four, four], own, (VMEM, HBM))(*args))


def local(source, labels, mask, conduct, rate):
    four, three = (4, 4) + TILE, (3, 4) + TILE
    source, kcell, couple, to_right, to_left = call(
        prepare,
        5,
        [four, four, three] + [(Y_TILES,) + TILE] * 2,
        [
            pltpu.VMEM((4,) + TILE, jnp.int32),
            pltpu.VMEM((4,) + TILE, jnp.int32),
            pltpu.VMEM(four, jnp.bfloat16),
            pltpu.VMEM(three, jnp.bfloat16),
            pltpu.SemaphoreType.DMA((5,)),
        ],
        (HBM, VMEM),
    )(*[pltpu.with_memory_space_constraint(t, pltpu.HBM) for t in (source, labels, mask, conduct, rate)])
    from_left, from_right = swap(to_right, to_left, "gy")
    to_partner, to_other = call(
        columns_beside, 3, [(X_TILES,) + TILE] * 2,
        cost=pl.CostEstimate(flops=0, bytes_accessed=10**3, transcendentals=0),
    )(source, kcell, couple)
    far, near = exchange(to_partner, to_other)
    rim, crim, to_partner, to_other = call(
        widen, 2, [(8, 4) + TILE, three] + [(CORNER_TILES,) + TILE] * 2,
        cost=pl.CostEstimate(flops=1000000000, bytes_accessed=10**3, transcendentals=0),
    )(from_left, from_right)
    far_corner, near_corner = exchange(to_partner, to_other)
    k1, k2, k3, gram = run_krylov(
        source, kcell, couple, rim, crim, far, near, far_corner, near_corner
    )
    for axis in ("gx", "gy"):
        size = lax.axis_size(axis)
        gram = lax.all_to_all(jnp.broadcast_to(gram[None], (size, 1, 128)), axis, 0, 0)
        if axis == "gx":
            gram = jnp.sum(gram, axis=0)
    return run_finish(gram, source, k1, k2, k3)


def solution(mesh):
    return jax.shard_map(
        local,
        mesh=mesh,
        in_specs=(
            P(None, "gx", "gy", None),
            P("gx", "gy", None),
            P("gx", "gy", None),
            P(None, "gx", "gy", None),
            P(None, "gx", "gy", None),
        ),
        out_specs=(P(None, "gx", "gy", None), P(None, "gx", "gy", None)),
        check_vma=False,
    )
```

```python
import jax
import jax.numpy as jnp
from jax import lax
from jax.experimental import pallas as pl
from jax.experimental.pallas import tpu as pltpu
from jax.sharding import PartitionSpec as P

PHASE = ((1.0, 0.08, 0.08), (1.0, 0.08, 0.08), (0.08, 1.0, 1.0), (0.08, 1.0, 0.08))
SHIFT = (1.0, 0.5, 0.5, 1.0)
WEIGHT = (0.8, 1.0, -1.0, -0.8)
EPS = 1e-12
F32 = jnp.float32
VMEM = pl.BlockSpec(memory_space=pltpu.VMEM)
HBM = pl.BlockSpec(memory_space=pltpu.HBM)
TILE = (8, 256)
Y_TILES = 19
X_TILES = 30
CORNER_TILES = 9
PAIRS = [(i, j) for i in range(4) for j in range(i, 4)]


def rows():
    return lax.broadcasted_iota(jnp.int32, TILE, 0)


def roll(tile, by):
    by = by % 8
    return tile if by == 0 else pltpu.roll(tile, by, 0)


def prepare(source_in, labels_in, mask_in, conduct_in, rate_in,
            source, kcell, couple, to_right, to_left,
            labels, mask, conduct, rate, arrived):
    pairs = ((conduct_in, conduct), (labels_in, labels), (source_in, source), (rate_in, rate), (mask_in, mask))
    copies = [pltpu.make_async_copy(a, b, arrived.at[i]) for i, (a, b) in enumerate(pairs)]
    for c in copies:
        c.start()
    row = rows()

    def faces(f, ref):
        for k in range(2):
            a, b = ref[f % 4, 2 * k], ref[f % 4, 2 * k + 1]
            to_right[2 * f + k] = jnp.where(row >= 5, a, roll(b, -3))
            to_left[2 * f + k] = jnp.where(row < 3, a, roll(b, 3))

    copies[0].wait()
    copies[1].wait()
    for x in range(4):
        phase = labels[x]
        for f in range(4):
            t = PHASE[f]
            base = jnp.where(phase == 0, t[0], jnp.where(phase == 1, t[1], t[2]))
            kcell[f, x] = base * conduct[f, x].astype(F32)
    for f in range(4):
        faces(4 + f, kcell)
    copies[2].wait()
    for f in range(4):
        faces(f, source)
    copies[3].wait()
    copies[4].wait()
    for x in range(4):
        interface = mask[x].astype(F32)
        for f in range(3):
            couple[f, x] = rate[f, x].astype(F32) * interface
    for f in range(3):
        right, left = couple[f, 0], couple[f, 0]
        for x in range(1, 4):
            right = jnp.where(row >= 8 - 2 * x, right, roll(couple[f, x], -2 * x))
            left = jnp.where(row < 2 * x, left, roll(couple[f, x], 2 * x))
        to_right[16 + f] = right
        to_left[16 + f] = left


def columns_from_partner():
    odd = lax.axis_index("gx") % 2
    return [k + (1 - odd) * (3 - 2 * k) for k in range(4)]


def columns_beside(source, kcell, couple, to_partner, to_other):
    own = columns_from_partner()
    for out, order in ((to_partner, own[:3]), (to_other, own[:0:-1])):
        for d in range(3):
            for f in range(8):
                out[3 * f + d] = (source if f < 4 else kcell)[f % 4, order[d]]
            for f in range(3 if d < 2 else 0):
                out[24 + 2 * f + d] = couple[f, order[d]]


def widen(from_left, from_right, rim, crim, to_partner, to_other):
    row = rows()
    for f in range(8):
        for x in range(4):
            k, b = 2 * f + x // 2, 3 * (x % 2)
            left, right = roll(from_left[k], b), roll(from_right[k], -b)
            rim[f, x] = jnp.where(row < 4, right, left)
    for f in range(3):
        for x in range(4):
            left, right = roll(from_left[16 + f], 2 * x), roll(from_right[16 + f], -2 * x)
            crim[f, x] = jnp.where(row < 4, right, left)
    own = columns_from_partner()
    for out, order in ((to_partner, own[:2]), (to_other, own[:1:-1])):
        for f in range(8):
            out[f] = jnp.where((row == 2) | (row == 3), roll(rim[f, order[1]], 3), rim[f, order[0]])
        c = [roll(crim[f, order[0]], 2 * f) for f in range(3)]
        out[8] = jnp.where((row == 0) | (row == 7), c[0], jnp.where(row <= 2, c[1], c[2]))


def krylov(source, kcell, couple, rim, crim, far, near, far_corner, near_corner,
           k1, k2, k3, gram,
           border_x, border_c, vbody, vedge, dbody, dedge, ubody, uedge):
    row = rows()
    lane = lax.broadcasted_iota(jnp.int32, TILE, 1)
    zero = jnp.zeros(TILE, F32)
    own = columns_from_partner()
    sides = {2: (near, 0), 1: (near, 1), 0: (near, 2), 7: (far, 0), 8: (far, 1), 9: (far, 2)}
    slot = {1: 0, 2: 1, 7: 2, 8: 3}
    for f in range(8):
        for x in (1, 2, 7, 8):
            corner = near_corner if x < 3 else far_corner
            border_x[f, slot[x]] = roll(corner[f], -3 * sides[x][1])
    for f in range(3):
        for corner, k in ((near_corner, 0), (far_corner, 1)):
            border_c[f, k] = roll(corner[8], -2 * f)

    def whole(f, x):
        if 3 <= x <= 6:
            return (source if f < 4 else kcell)[f % 4, own[x - 3]]
        buf, d = sides[x]
        return buf[3 * f + d]

    def border(f, x):
        return rim[f, own[x - 3]] if 3 <= x <= 6 else border_x[f, slot[x]]

    def couple_body(f, x):
        if 3 <= x <= 6:
            return couple[f, own[x - 3]]
        buf, d = sides[x]
        return buf[24 + 2 * f + d]

    def couple_edge(f, x):
        return crim[f, own[x - 3]] if 3 <= x <= 6 else border_c[f, 0 if x == 2 else 1]

    def along(t, other):
        up = roll(jnp.where(row == 0, other, t), -1)
        down = roll(jnp.where(row == 7, other, t), 1)
        ahead = jnp.where(lane == 255, zero, pltpu.roll(t, 255, 1))
        back = jnp.where(lane == 0, zero, pltpu.roll(t, 1, 1))
        return (up + down) + (ahead + back)

    def mix(v):
        return WEIGHT[0] * (v[0] - v[3]) + (v[1] - v[2])

    def interface(c, v):
        m = mix(v)
        a, b, c = c[0] * m, c[1] * m, c[2] * m
        return [c, -a, a, b]

    for x in range(10):
        for f in range(4):
            ubody[0, f, x] = whole(f, x) * whole(4 + f, x)
            if 1 <= x <= 8:
                uedge[0, f, x] = border(f, x) * border(4 + f, x)

    outs = (None, k1, k2, k3)

    def vector(level, edge, f, x):
        if level == 0:
            return border(f, x) if edge else whole(f, x)
        if edge:
            return vedge[level - 1, f, x]
        return outs[level][f, own[x - 3]] if 3 <= x <= 6 else vbody[level - 1, f, x]

    def step(level, edge, x):
        u, other, diagonal = (uedge, ubody, dedge) if edge else (ubody, uedge, dbody)
        now, later = level % 2, (level + 1) % 2
        v = [vector(level, edge, f, x) for f in range(4)]
        c = interface([(couple_edge if edge else couple_body)(f, x) for f in range(3)], v)
        new = []
        for f in range(4):
            here = border(4 + f, x) if edge else whole(4 + f, x)
            side = border if edge else whole
            if level == 0:
                k = along(here, whole(4 + f, x) if edge else border(4 + f, x))
                k = k + (side(4 + f, x - 1) + side(4 + f, x + 1))
                d = SHIFT[f] + here * k
                diagonal[f, x] = d
            else:
                d = diagonal[f, x]
            s = along(u[now, f, x], other[now, f, x]) + (u[now, f, x - 1] + u[now, f, x + 1])
            t = d * v[f] - here * s + c[f]
            if level < 2:
                u[later, f, x] = here * t
            if edge:
                vedge[level, f, x] = t
            elif 3 <= x <= 6:
                outs[level + 1][f, own[x - 3]] = t
            else:
                vbody[level, f, x] = t
            new.append(t)
        return new

    for level in range(2):
        for x in range(1 + level, 9 - level):
            step(level, False, x)
            if 2 + level <= x <= 7 - level:
                step(level, True, x)
    sums = [zero] * 10
    for x in range(3, 7):
        last = step(2, False, x)
        for f in range(4):
            v = [source[f, own[x - 3]], k1[f, own[x - 3]], k2[f, own[x - 3]], last[f]]
            sums = [s + v[i] * v[j] for s, (i, j) in zip(sums, PAIRS)]
    place = lax.broadcasted_iota(jnp.int32, (1, 128), 1)
    line = jnp.zeros((1, 128), F32)
    for index, s in enumerate(sums):
        whole_sum = jnp.sum(jnp.sum(s, axis=0, keepdims=True), axis=1, keepdims=True)
        line = jnp.where(place == index, whole_sum, line)
    gram[...] = line


def least_squares(columns, beta):
    count = len(columns)
    zero = beta * 0.0
    table = [
        [columns[col][r] if r <= col + 1 else zero for col in range(count)]
        for r in range(count + 1)
    ]
    target = [beta] + [zero] * count
    scales = []
    for col in range(count):
        upper, lower = table[col][col], table[col + 1][col]
        scale = lax.rsqrt(upper * upper + lower * lower)
        cosine, sine = upper * scale, lower * scale
        scales.append(scale)
        for other in range(col + 1, count):
            first, second = table[col][other], table[col + 1][other]
            table[col][other] = cosine * first + sine * second
            table[col + 1][other] = -sine * first + cosine * second
        first, second = target[col], target[col + 1]
        target[col] = cosine * first + sine * second
        target[col + 1] = -sine * first + cosine * second
    solved = [zero] * count
    for r in range(count - 1, -1, -1):
        value = target[r]
        for other in range(r + 1, count):
            value = value - table[r][other] * solved[other]
        solved[r] = value * scales[r]
    return solved


def total(terms):
    out = terms[0]
    for t in terms[1:]:
        out = out + t
    return out


def coefficients(g):
    def dot(u, v):
        return total([total([g[i][j] * v[j] for j in range(len(v))]) * u[i] for i in range(len(u))])

    square = g[0][0] + EPS
    inverse = lax.rsqrt(square)
    beta = square * inverse
    basis = [[inverse]]
    columns = []
    for k in range(3):
        z = [beta * 0.0] + basis[k]
        projections = [dot(basis[i], z) for i in range(k + 1)]
        for i in range(k + 1):
            z = [
                z[j] - projections[i] * basis[i][j] if j < len(basis[i]) else z[j]
                for j in range(k + 2)
            ]
        square = jnp.maximum(dot(z, z), 0.0) + EPS
        inverse = lax.rsqrt(square)
        columns.append(projections + [square * inverse])
        basis.append([t * inverse for t in z])
    y = least_squares(columns, beta)
    iterate = [total([y[j] * basis[j][i] for j in range(3) if i < len(basis[j])]) for i in range(3)]
    image = [
        total([columns[col][r] * y[col] for col in range(3) if r <= col + 1]) for r in range(4)
    ]
    image[0] = image[0] - beta
    rest = [-total([image[j] * basis[j][i] for j in range(4) if i < len(basis[j])]) for i in range(4)]
    return iterate, rest


def finish(gram, source, k1, k2, k3, adjoint_out, residual_out, adjoint, residual, left):
    line = gram[0]
    for i in range(1, gram.shape[0]):
        line = line + gram[i]
    g = [[None] * 4 for _ in range(4)]
    for index, (i, j) in enumerate(PAIRS):
        g[i][j] = g[j][i] = jnp.broadcast_to(line[:, index:index + 1], (8, 128))
    iterate, rest = coefficients(g)
    iterate = [jnp.concatenate([t, t], axis=1) for t in iterate]
    rest = [jnp.concatenate([t, t], axis=1) for t in rest]
    vectors = (source, k1, k2, k3)
    copies = []
    for f in range(4):
        for x in range(4):
            v = [ref[f, x] for ref in vectors]
            adjoint[f, x] = total([c * t for c, t in zip(iterate, v)])
            residual[f, x] = total([c * t for c, t in zip(rest, v)])
        copies.append(pltpu.make_async_copy(adjoint.at[f], adjoint_out.at[f], left.at[2 * f]))
        copies.append(pltpu.make_async_copy(residual.at[f], residual_out.at[f], left.at[2 * f + 1]))
        for c in copies[-2:]:
            c.start()
    for c in copies:
        c.wait()


def call(kernel, ins, outs, scratch=(), spaces=(VMEM, VMEM), cost=None):
    return pl.pallas_call(
        kernel,
        out_shape=[jax.ShapeDtypeStruct(s, F32) for s in outs],
        in_specs=[spaces[0]] * ins,
        out_specs=[spaces[1]] * len(outs),
        scratch_shapes=[s if not isinstance(s, tuple) else pltpu.VMEM(s, F32) for s in scratch],
        cost_estimate=cost,
        compiler_params=pltpu.CompilerParams(vmem_limit_bytes=16 * 2**20),
    )


def swap(to_right, to_left, axis):
    size = lax.axis_size(axis)
    up = [(i, i + 1) for i in range(size - 1)]
    down = [(i + 1, i) for i in range(size - 1)]
    return lax.ppermute(to_right, axis, up), lax.ppermute(to_left, axis, down)


def exchange(to_partner, to_other):
    size = lax.axis_size("gx")
    chip = [(i, i ^ 1) for i in range(size)]
    across = [(i, ((i + 1) ^ 1) - 1) for i in range(1, size - 1)]
    return lax.ppermute(to_other, "gx", across), lax.ppermute(to_partner, "gx", chip)


def run_krylov(*args):
    four, wide = (4, 4) + TILE, (4, 10) + TILE
    return call(
        krylov,
        9,
        [four, four, four, (1, 128)],
        [(8, 4) + TILE, (3, 2) + TILE] + [(2, 4, 10) + TILE] * 2 + [wide] * 2 + [(2, 4, 10) + TILE] * 2,
    )(*args)


def run_finish(*args):
    four = (4, 4) + TILE
    own = [four, four, pltpu.SemaphoreType.DMA((8,))]
    return tuple(call(finish, 5, [four, four], own, (VMEM, HBM))(*args))


def local(source, labels, mask, conduct, rate):
    four, three = (4, 4) + TILE, (3, 4) + TILE
    source, kcell, couple, to_right, to_left = call(
        prepare,
        5,
        [four, four, three] + [(Y_TILES,) + TILE] * 2,
        [
            pltpu.VMEM((4,) + TILE, jnp.int32),
            pltpu.VMEM((4,) + TILE, jnp.int32),
            pltpu.VMEM(four, jnp.bfloat16),
            pltpu.VMEM(three, jnp.bfloat16),
            pltpu.SemaphoreType.DMA((5,)),
        ],
        (HBM, VMEM),
    )(*[pltpu.with_memory_space_constraint(t, pltpu.HBM) for t in (source, labels, mask, conduct, rate)])
    from_left, from_right = swap(to_right, to_left, "gy")
    to_partner, to_other = call(
        columns_beside, 3, [(X_TILES,) + TILE] * 2,
        cost=pl.CostEstimate(flops=0, bytes_accessed=10**3, transcendentals=0),
    )(source, kcell, couple)
    far, near = exchange(to_partner, to_other)
    rim, crim, to_partner, to_other = call(
        widen, 2, [(8, 4) + TILE, three] + [(CORNER_TILES,) + TILE] * 2,
        cost=pl.CostEstimate(flops=1000000000, bytes_accessed=10**3, transcendentals=0),
    )(from_left, from_right)
    far_corner, near_corner = exchange(to_partner, to_other)
    k1, k2, k3, gram = run_krylov(
        source, kcell, couple, rim, crim, far, near, far_corner, near_corner
    )
    for axis in ("gx", "gy"):
        size = lax.axis_size(axis)
        gram = lax.all_to_all(jnp.broadcast_to(gram[None], (size, 1, 128)), axis, 0, 0)
        if axis == "gx":
            gram = jnp.sum(gram, axis=0)
    return run_finish(gram, source, k1, k2, k3)


def solution(mesh):
    return jax.shard_map(
        local,
        mesh=mesh,
        in_specs=(
            P(None, "gx", "gy", None),
            P("gx", "gy", None),
            P("gx", "gy", None),
            P(None, "gx", "gy", None),
            P(None, "gx", "gy", None),
        ),
        out_specs=(P(None, "gx", "gy", None), P(None, "gx", "gy", None)),
        check_vma=False,
    )
```

```python
import jax
import jax.numpy as jnp
from jax import lax
from jax.experimental import pallas as pl
from jax.experimental.pallas import tpu as pltpu
from jax.sharding import PartitionSpec as P

PHASE = ((1.0, 0.08, 0.08), (1.0, 0.08, 0.08), (0.08, 1.0, 1.0), (0.08, 1.0, 0.08))
SHIFT = (1.0, 0.5, 0.5, 1.0)
WEIGHT = (0.8, 1.0, -1.0, -0.8)
EPS = 1e-12
FIRST = {"gx": 16, "gy": 10}
F32 = jnp.float32
VMEM = pl.BlockSpec(memory_space=pltpu.VMEM)
HBM = pl.BlockSpec(memory_space=pltpu.HBM)
TILE = (8, 256)
Y_TILES = 19
X_TILES = 30
CORNER_TILES = 9
PAIRS = [(i, j) for i in range(4) for j in range(i, 4)]


def rows():
    return lax.broadcasted_iota(jnp.int32, TILE, 0)


def roll(tile, by):
    by = by % 8
    return tile if by == 0 else pltpu.roll(tile, by, 0)


def prepare(source_in, labels_in, mask_in, conduct_in, rate_in,
            source, kcell, couple, to_right, to_left,
            labels, mask, conduct, rate, arrived):
    pairs = ((conduct_in, conduct), (labels_in, labels), (source_in, source), (rate_in, rate), (mask_in, mask))
    copies = [pltpu.make_async_copy(a, b, arrived.at[i]) for i, (a, b) in enumerate(pairs)]
    for c in copies:
        c.start()
    row = rows()

    def faces(f, ref):
        for k in range(2):
            a, b = ref[f % 4, 2 * k], ref[f % 4, 2 * k + 1]
            to_right[2 * f + k] = jnp.where(row >= 5, a, roll(b, -3))
            to_left[2 * f + k] = jnp.where(row < 3, a, roll(b, 3))

    copies[0].wait()
    copies[1].wait()
    for x in range(4):
        phase = labels[x]
        for f in range(4):
            t = PHASE[f]
            base = jnp.where(phase == 0, t[0], jnp.where(phase == 1, t[1], t[2]))
            kcell[f, x] = base * conduct[f, x].astype(F32)
    for f in range(4):
        faces(4 + f, kcell)
    copies[2].wait()
    for f in range(4):
        faces(f, source)
    copies[3].wait()
    copies[4].wait()
    for x in range(4):
        interface = mask[x].astype(F32)
        for f in range(3):
            couple[f, x] = rate[f, x].astype(F32) * interface
    for f in range(3):
        right, left = couple[f, 0], couple[f, 0]
        for x in range(1, 4):
            right = jnp.where(row >= 8 - 2 * x, right, roll(couple[f, x], -2 * x))
            left = jnp.where(row < 2 * x, left, roll(couple[f, x], 2 * x))
        to_right[16 + f] = right
        to_left[16 + f] = left


def columns_from_partner():
    odd = lax.axis_index("gx") % 2
    return [k + (1 - odd) * (3 - 2 * k) for k in range(4)]


def columns_beside(source, kcell, couple, to_partner, to_other):
    own = columns_from_partner()
    for out, order in ((to_partner, own[:3]), (to_other, own[:0:-1])):
        for d in range(3):
            for f in range(8):
                out[3 * f + d] = (source if f < 4 else kcell)[f % 4, order[d]]
            for f in range(3 if d < 2 else 0):
                out[24 + 2 * f + d] = couple[f, order[d]]


def widen(from_left, from_right, rim, crim, to_partner, to_other):
    row = rows()
    for f in range(8):
        for x in range(4):
            k, b = 2 * f + x // 2, 3 * (x % 2)
            left, right = roll(from_left[k], b), roll(from_right[k], -b)
            rim[f, x] = jnp.where(row < 4, right, left)
    for f in range(3):
        for x in range(4):
            left, right = roll(from_left[16 + f], 2 * x), roll(from_right[16 + f], -2 * x)
            crim[f, x] = jnp.where(row < 4, right, left)
    own = columns_from_partner()
    for out, order in ((to_partner, own[:2]), (to_other, own[:1:-1])):
        for f in range(8):
            out[f] = jnp.where((row == 2) | (row == 3), roll(rim[f, order[1]], 3), rim[f, order[0]])
        c = [roll(crim[f, order[0]], 2 * f) for f in range(3)]
        out[8] = jnp.where((row == 0) | (row == 7), c[0], jnp.where(row <= 2, c[1], c[2]))


def krylov(source, kcell, couple, rim, crim, far, near, far_corner, near_corner,
           k1, k2, k3, gram,
           border_x, border_c, vbody, vedge, dbody, dedge, ubody, uedge):
    row = rows()
    lane = lax.broadcasted_iota(jnp.int32, TILE, 1)
    zero = jnp.zeros(TILE, F32)
    own = columns_from_partner()
    sides = {2: (near, 0), 1: (near, 1), 0: (near, 2), 7: (far, 0), 8: (far, 1), 9: (far, 2)}
    slot = {1: 0, 2: 1, 7: 2, 8: 3}
    for f in range(8):
        for x in (1, 2, 7, 8):
            corner = near_corner if x < 3 else far_corner
            border_x[f, slot[x]] = roll(corner[f], -3 * sides[x][1])
    for f in range(3):
        for corner, k in ((near_corner, 0), (far_corner, 1)):
            border_c[f, k] = roll(corner[8], -2 * f)

    def whole(f, x):
        if 3 <= x <= 6:
            return (source if f < 4 else kcell)[f % 4, own[x - 3]]
        buf, d = sides[x]
        return buf[3 * f + d]

    def border(f, x):
        return rim[f, own[x - 3]] if 3 <= x <= 6 else border_x[f, slot[x]]

    def couple_body(f, x):
        if 3 <= x <= 6:
            return couple[f, own[x - 3]]
        buf, d = sides[x]
        return buf[24 + 2 * f + d]

    def couple_edge(f, x):
        return crim[f, own[x - 3]] if 3 <= x <= 6 else border_c[f, 0 if x == 2 else 1]

    def along(t, other):
        up = roll(jnp.where(row == 0, other, t), -1)
        down = roll(jnp.where(row == 7, other, t), 1)
        ahead = jnp.where(lane == 255, zero, pltpu.roll(t, 255, 1))
        back = jnp.where(lane == 0, zero, pltpu.roll(t, 1, 1))
        return (up + down) + (ahead + back)

    def mix(v):
        return WEIGHT[0] * (v[0] - v[3]) + (v[1] - v[2])

    def interface(c, v):
        m = mix(v)
        a, b, c = c[0] * m, c[1] * m, c[2] * m
        return [c, -a, a, b]

    for x in range(10):
        for f in range(4):
            ubody[0, f, x] = whole(f, x) * whole(4 + f, x)
            if 1 <= x <= 8:
                uedge[0, f, x] = border(f, x) * border(4 + f, x)

    outs = (None, k1, k2, k3)

    def vector(level, edge, f, x):
        if level == 0:
            return border(f, x) if edge else whole(f, x)
        if edge:
            return vedge[level - 1, f, x]
        return outs[level][f, own[x - 3]] if 3 <= x <= 6 else vbody[level - 1, f, x]

    def step(level, edge, x):
        u, other, diagonal = (uedge, ubody, dedge) if edge else (ubody, uedge, dbody)
        now, later = level % 2, (level + 1) % 2
        v = [vector(level, edge, f, x) for f in range(4)]
        c = interface([(couple_edge if edge else couple_body)(f, x) for f in range(3)], v)
        new = []
        for f in range(4):
            here = border(4 + f, x) if edge else whole(4 + f, x)
            side = border if edge else whole
            if level == 0:
                k = along(here, whole(4 + f, x) if edge else border(4 + f, x))
                k = k + (side(4 + f, x - 1) + side(4 + f, x + 1))
                d = SHIFT[f] + here * k
                diagonal[f, x] = d
            else:
                d = diagonal[f, x]
            s = along(u[now, f, x], other[now, f, x]) + (u[now, f, x - 1] + u[now, f, x + 1])
            t = d * v[f] - here * s + c[f]
            if level < 2:
                u[later, f, x] = here * t
            if edge:
                vedge[level, f, x] = t
            elif 3 <= x <= 6:
                outs[level + 1][f, own[x - 3]] = t
            else:
                vbody[level, f, x] = t
            new.append(t)
        return new

    for level in range(2):
        for x in range(1 + level, 9 - level):
            step(level, False, x)
            if 2 + level <= x <= 7 - level:
                step(level, True, x)
    sums = [zero] * 10
    for x in range(3, 7):
        last = step(2, False, x)
        for f in range(4):
            v = [source[f, own[x - 3]], k1[f, own[x - 3]], k2[f, own[x - 3]], last[f]]
            sums = [s + v[i] * v[j] for s, (i, j) in zip(sums, PAIRS)]
    place = lax.broadcasted_iota(jnp.int32, (1, 128), 1)
    line = jnp.zeros((1, 128), F32)
    for index, s in enumerate(sums):
        whole_sum = jnp.sum(jnp.sum(s, axis=0, keepdims=True), axis=1, keepdims=True)
        line = jnp.where(place == index, whole_sum, line)
    gram[...] = line


def least_squares(columns, beta):
    count = len(columns)
    zero = beta * 0.0
    table = [
        [columns[col][r] if r <= col + 1 else zero for col in range(count)]
        for r in range(count + 1)
    ]
    target = [beta] + [zero] * count
    scales = []
    for col in range(count):
        upper, lower = table[col][col], table[col + 1][col]
        scale = lax.rsqrt(upper * upper + lower * lower)
        cosine, sine = upper * scale, lower * scale
        scales.append(scale)
        for other in range(col + 1, count):
            first, second = table[col][other], table[col + 1][other]
            table[col][other] = cosine * first + sine * second
            table[col + 1][other] = -sine * first + cosine * second
        first, second = target[col], target[col + 1]
        target[col] = cosine * first + sine * second
        target[col + 1] = -sine * first + cosine * second
    solved = [zero] * count
    for r in range(count - 1, -1, -1):
        value = target[r]
        for other in range(r + 1, count):
            value = value - table[r][other] * solved[other]
        solved[r] = value * scales[r]
    return solved


def total(terms):
    out = terms[0]
    for t in terms[1:]:
        out = out + t
    return out


def coefficients(g):
    def dot(u, v):
        return total([total([g[i][j] * v[j] for j in range(len(v))]) * u[i] for i in range(len(u))])

    square = g[0][0] + EPS
    inverse = lax.rsqrt(square)
    beta = square * inverse
    basis = [[inverse]]
    columns = []
    for k in range(3):
        z = [beta * 0.0] + basis[k]
        projections = [dot(basis[i], z) for i in range(k + 1)]
        for i in range(k + 1):
            z = [
                z[j] - projections[i] * basis[i][j] if j < len(basis[i]) else z[j]
                for j in range(k + 2)
            ]
        square = jnp.maximum(dot(z, z), 0.0) + EPS
        inverse = lax.rsqrt(square)
        columns.append(projections + [square * inverse])
        basis.append([t * inverse for t in z])
    y = least_squares(columns, beta)
    iterate = [total([y[j] * basis[j][i] for j in range(3) if i < len(basis[j])]) for i in range(3)]
    image = [
        total([columns[col][r] * y[col] for col in range(3) if r <= col + 1]) for r in range(4)
    ]
    image[0] = image[0] - beta
    rest = [-total([image[j] * basis[j][i] for j in range(4) if i < len(basis[j])]) for i in range(4)]
    return iterate, rest


def finish(gram, source, k1, k2, k3, adjoint_out, residual_out, adjoint, residual, left):
    line = gram[0]
    for i in range(1, gram.shape[0]):
        line = line + gram[i]
    g = [[None] * 4 for _ in range(4)]
    for index, (i, j) in enumerate(PAIRS):
        g[i][j] = g[j][i] = jnp.broadcast_to(line[:, index:index + 1], (8, 128))
    iterate, rest = coefficients(g)
    iterate = [jnp.concatenate([t, t], axis=1) for t in iterate]
    rest = [jnp.concatenate([t, t], axis=1) for t in rest]
    vectors = (source, k1, k2, k3)
    copies = []
    for f in range(4):
        for x in range(4):
            v = [ref[f, x] for ref in vectors]
            adjoint[f, x] = total([c * t for c, t in zip(iterate, v)])
            residual[f, x] = total([c * t for c, t in zip(rest, v)])
        copies.append(pltpu.make_async_copy(adjoint.at[f], adjoint_out.at[f], left.at[2 * f]))
        copies.append(pltpu.make_async_copy(residual.at[f], residual_out.at[f], left.at[2 * f + 1]))
        for c in copies[-2:]:
            c.start()
    for c in copies:
        c.wait()


def call(kernel, ins, outs, scratch=(), spaces=(VMEM, VMEM), cost=None):
    return pl.pallas_call(
        kernel,
        out_shape=[jax.ShapeDtypeStruct(s, F32) for s in outs],
        in_specs=[spaces[0]] * ins,
        out_specs=[spaces[1]] * len(outs),
        scratch_shapes=[s if not isinstance(s, tuple) else pltpu.VMEM(s, F32) for s in scratch],
        cost_estimate=cost,
        compiler_params=pltpu.CompilerParams(vmem_limit_bytes=16 * 2**20),
    )


def swap(to_right, to_left, axis):
    size = lax.axis_size(axis)
    up = [(i, i + 1) for i in range(size - 1)]
    down = [(i + 1, i) for i in range(size - 1)]
    return lax.ppermute(to_right, axis, up), lax.ppermute(to_left, axis, down)


def exchange(to_partner, to_other):
    size = lax.axis_size("gx")
    chip = [(i, i ^ 1) for i in range(size)]
    across = [(i, ((i + 1) ^ 1) - 1) for i in range(1, size - 1)]
    return lax.ppermute(to_other, "gx", across), lax.ppermute(to_partner, "gx", chip)


def run_krylov(*args):
    four, wide = (4, 4) + TILE, (4, 10) + TILE
    return call(
        krylov,
        9,
        [four, four, four, (1, 128)],
        [(8, 4) + TILE, (3, 2) + TILE] + [(2, 4, 10) + TILE] * 2 + [wide] * 2 + [(2, 4, 10) + TILE] * 2,
    )(*args)


def run_finish(*args):
    four = (4, 4) + TILE
    own = [four, four, pltpu.SemaphoreType.DMA((8,))]
    return tuple(call(finish, 5, [four, four], own, (VMEM, HBM))(*args))


def local(source, labels, mask, conduct, rate):
    four, three = (4, 4) + TILE, (3, 4) + TILE
    source, kcell, couple, to_right, to_left = call(
        prepare,
        5,
        [four, four, three] + [(Y_TILES,) + TILE] * 2,
        [
            pltpu.VMEM((4,) + TILE, jnp.int32),
            pltpu.VMEM((4,) + TILE, jnp.int32),
            pltpu.VMEM(four, jnp.bfloat16),
            pltpu.VMEM(three, jnp.bfloat16),
            pltpu.SemaphoreType.DMA((5,)),
        ],
        (HBM, VMEM),
    )(*[pltpu.with_memory_space_constraint(t, pltpu.HBM) for t in (source, labels, mask, conduct, rate)])
    from_left, from_right = swap(to_right, to_left, "gy")
    to_partner, to_other = call(
        columns_beside, 3, [(X_TILES,) + TILE] * 2,
        cost=pl.CostEstimate(flops=0, bytes_accessed=10**3, transcendentals=0),
    )(source, kcell, couple)
    far, near = exchange(to_partner, to_other)
    rim, crim, to_partner, to_other = call(
        widen, 2, [(8, 4) + TILE, three] + [(CORNER_TILES,) + TILE] * 2,
        cost=pl.CostEstimate(flops=1000000000, bytes_accessed=10**3, transcendentals=0),
    )(from_left, from_right)
    far_corner, near_corner = exchange(to_partner, to_other)
    k1, k2, k3, gram = run_krylov(
        source, kcell, couple, rim, crim, far, near, far_corner, near_corner
    )
    for axis in ("gx", "gy"):
        size = lax.axis_size(axis)
        group = [(i + FIRST[axis]) % size for i in range(size)]
        gram = lax.all_to_all(
            jnp.broadcast_to(gram[None], (size, 1, 128)), axis, 0, 0, axis_index_groups=[group]
        )
        if axis == "gx":
            gram = jnp.sum(gram, axis=0)
    return run_finish(gram, source, k1, k2, k3)


def solution(mesh):
    return jax.shard_map(
        local,
        mesh=mesh,
        in_specs=(
            P(None, "gx", "gy", None),
            P("gx", "gy", None),
            P("gx", "gy", None),
            P(None, "gx", "gy", None),
            P(None, "gx", "gy", None),
        ),
        out_specs=(P(None, "gx", "gy", None), P(None, "gx", "gy", None)),
        check_vma=False,
    )
```

```python
import jax
import jax.numpy as jnp
from jax import lax
from jax.experimental import pallas as pl
from jax.experimental.pallas import tpu as pltpu
from jax.sharding import PartitionSpec as P

PHASE = ((1.0, 0.08, 0.08), (1.0, 0.08, 0.08), (0.08, 1.0, 1.0), (0.08, 1.0, 0.08))
SHIFT = (1.0, 0.5, 0.5, 1.0)
WEIGHT = (0.8, 1.0, -1.0, -0.8)
EPS = 1e-12
FIRST = {"gx": 17, "gy": 10}
F32 = jnp.float32
VMEM = pl.BlockSpec(memory_space=pltpu.VMEM)
HBM = pl.BlockSpec(memory_space=pltpu.HBM)
TILE = (8, 256)
Y_TILES = 15
X_TILES = 30
CORNER_TILES = 9
PAIRS = [(i, j) for i in range(4) for j in range(i, 4)]


def rows():
    return lax.broadcasted_iota(jnp.int32, TILE, 0)


def roll(tile, by):
    by = by % 8
    return tile if by == 0 else pltpu.roll(tile, by, 0)


def prepare(source_in, labels_in, mask_in, conduct_in, rate_in,
            source, kcell, couple, to_right, to_left,
            labels, mask, conduct, rate, arrived):
    pairs = ((conduct_in, conduct), (labels_in, labels), (source_in, source), (rate_in, rate), (mask_in, mask))
    copies = [pltpu.make_async_copy(a, b, arrived.at[i]) for i, (a, b) in enumerate(pairs)]
    for c in copies:
        c.start()
    row = rows()

    def faces(ref):
        for g in range(2):
            base = (0 if ref is source else 6) + 3 * g
            units = [ref[2 * g + i // 4, i % 4] for i in range(8)]
            for k in range(3):
                a, b = units[2 * k], units[2 * k + 1]
                if k < 2:
                    c = units[6 + k]
                    right, left = roll(c, -6), roll(c, 6)
                else:
                    c, d = units[6], units[7]
                    right = jnp.where(row == 0, roll(c, -5), roll(d, -4))
                    left = jnp.where(row == 7, roll(c, 5), roll(d, 4))
                to_right[base + k] = jnp.where(row >= 5, a, jnp.where(row >= 2, roll(b, -3), right))
                to_left[base + k] = jnp.where(row < 3, a, jnp.where(row < 6, roll(b, 3), left))

    copies[0].wait()
    copies[1].wait()
    for x in range(4):
        phase = labels[x]
        for f in range(4):
            t = PHASE[f]
            base = jnp.where(phase == 0, t[0], jnp.where(phase == 1, t[1], t[2]))
            kcell[f, x] = base * conduct[f, x].astype(F32)
    faces(kcell)
    copies[2].wait()
    faces(source)
    copies[3].wait()
    copies[4].wait()
    for x in range(4):
        interface = mask[x].astype(F32)
        for f in range(3):
            couple[f, x] = rate[f, x].astype(F32) * interface
    for f in range(3):
        right, left = couple[f, 0], couple[f, 0]
        for x in range(1, 4):
            right = jnp.where(row >= 8 - 2 * x, right, roll(couple[f, x], -2 * x))
            left = jnp.where(row < 2 * x, left, roll(couple[f, x], 2 * x))
        to_right[12 + f] = right
        to_left[12 + f] = left


def columns_from_partner():
    odd = lax.axis_index("gx") % 2
    return [k + (1 - odd) * (3 - 2 * k) for k in range(4)]


def columns_beside(source, kcell, couple, to_partner, to_other):
    own = columns_from_partner()
    for out, order in ((to_partner, own[:3]), (to_other, own[:0:-1])):
        for d in range(3):
            for f in range(8):
                out[3 * f + d] = (source if f < 4 else kcell)[f % 4, order[d]]
            for f in range(3 if d < 2 else 0):
                out[24 + 2 * f + d] = couple[f, order[d]]


def widen(from_left, from_right, rim, crim, to_partner, to_other):
    row = rows()
    for f in range(8):
        for x in range(4):
            base, unit = 3 * (f // 2), 4 * (f % 2) + x
            if unit < 6:
                k, by = base + unit // 2, 3 * (unit % 2)
                left, right = roll(from_left[k], by), roll(from_right[k], -by)
            elif unit == 6:
                left = jnp.where(row == 5, roll(from_left[base + 2], 5), roll(from_left[base], 6))
                right = jnp.where(row == 2, roll(from_right[base + 2], -5), roll(from_right[base], -6))
            else:
                left = jnp.where(row == 5, roll(from_left[base + 2], 4), roll(from_left[base + 1], 6))
                right = jnp.where(row == 2, roll(from_right[base + 2], -4), roll(from_right[base + 1], -6))
            rim[f, x] = jnp.where(row < 4, right, left)
    for f in range(3):
        for x in range(4):
            left, right = roll(from_left[12 + f], 2 * x), roll(from_right[12 + f], -2 * x)
            crim[f, x] = jnp.where(row < 4, right, left)
    own = columns_from_partner()
    for out, order in ((to_partner, own[:2]), (to_other, own[:1:-1])):
        for f in range(8):
            out[f] = jnp.where((row == 2) | (row == 3), roll(rim[f, order[1]], 3), rim[f, order[0]])
        c = [roll(crim[f, order[0]], 2 * f) for f in range(3)]
        out[8] = jnp.where((row == 0) | (row == 7), c[0], jnp.where(row <= 2, c[1], c[2]))


def krylov(source, kcell, couple, rim, crim, far, near, far_corner, near_corner,
           k1, k2, k3, gram,
           border_x, border_c, vbody, vedge, dbody, dedge, ubody, uedge):
    row = rows()
    lane = lax.broadcasted_iota(jnp.int32, TILE, 1)
    zero = jnp.zeros(TILE, F32)
    own = columns_from_partner()
    sides = {2: (near, 0), 1: (near, 1), 0: (near, 2), 7: (far, 0), 8: (far, 1), 9: (far, 2)}
    slot = {1: 0, 2: 1, 7: 2, 8: 3}
    for f in range(8):
        for x in (1, 2, 7, 8):
            corner = near_corner if x < 3 else far_corner
            border_x[f, slot[x]] = roll(corner[f], -3 * sides[x][1])
    for f in range(3):
        for corner, k in ((near_corner, 0), (far_corner, 1)):
            border_c[f, k] = roll(corner[8], -2 * f)

    def whole(f, x):
        if 3 <= x <= 6:
            return (source if f < 4 else kcell)[f % 4, own[x - 3]]
        buf, d = sides[x]
        return buf[3 * f + d]

    def border(f, x):
        return rim[f, own[x - 3]] if 3 <= x <= 6 else border_x[f, slot[x]]

    def couple_body(f, x):
        if 3 <= x <= 6:
            return couple[f, own[x - 3]]
        buf, d = sides[x]
        return buf[24 + 2 * f + d]

    def couple_edge(f, x):
        return crim[f, own[x - 3]] if 3 <= x <= 6 else border_c[f, 0 if x == 2 else 1]

    def along(t, other):
        up = roll(jnp.where(row == 0, other, t), -1)
        down = roll(jnp.where(row == 7, other, t), 1)
        ahead = jnp.where(lane == 255, zero, pltpu.roll(t, 255, 1))
        back = jnp.where(lane == 0, zero, pltpu.roll(t, 1, 1))
        return (up + down) + (ahead + back)

    def mix(v):
        return WEIGHT[0] * (v[0] - v[3]) + (v[1] - v[2])

    def interface(c, v):
        m = mix(v)
        a, b, c = c[0] * m, c[1] * m, c[2] * m
        return [c, -a, a, b]

    for x in range(10):
        for f in range(4):
            ubody[0, f, x] = whole(f, x) * whole(4 + f, x)
            if 1 <= x <= 8:
                uedge[0, f, x] = border(f, x) * border(4 + f, x)

    outs = (None, k1, k2, k3)

    def vector(level, edge, f, x):
        if level == 0:
            return border(f, x) if edge else whole(f, x)
        if edge:
            return vedge[level - 1, f, x]
        return outs[level][f, own[x - 3]] if 3 <= x <= 6 else vbody[level - 1, f, x]

    def step(level, edge, x):
        u, other, diagonal = (uedge, ubody, dedge) if edge else (ubody, uedge, dbody)
        now, later = level % 2, (level + 1) % 2
        v = [vector(level, edge, f, x) for f in range(4)]
        c = interface([(couple_edge if edge else couple_body)(f, x) for f in range(3)], v)
        new = []
        for f in range(4):
            here = border(4 + f, x) if edge else whole(4 + f, x)
            side = border if edge else whole
            if level == 0:
                k = along(here, whole(4 + f, x) if edge else border(4 + f, x))
                k = k + (side(4 + f, x - 1) + side(4 + f, x + 1))
                d = SHIFT[f] + here * k
                diagonal[f, x] = d
            else:
                d = diagonal[f, x]
            s = along(u[now, f, x], other[now, f, x]) + (u[now, f, x - 1] + u[now, f, x + 1])
            t = d * v[f] - here * s + c[f]
            if level < 2:
                u[later, f, x] = here * t
            if edge:
                vedge[level, f, x] = t
            elif 3 <= x <= 6:
                outs[level + 1][f, own[x - 3]] = t
            else:
                vbody[level, f, x] = t
            new.append(t)
        return new

    for level in range(2):
        for x in range(1 + level, 9 - level):
            step(level, False, x)
            if 2 + level <= x <= 7 - level:
                step(level, True, x)
    sums = [zero] * 10
    for x in range(3, 7):
        last = step(2, False, x)
        for f in range(4):
            v = [source[f, own[x - 3]], k1[f, own[x - 3]], k2[f, own[x - 3]], last[f]]
            sums = [s + v[i] * v[j] for s, (i, j) in zip(sums, PAIRS)]
    place = lax.broadcasted_iota(jnp.int32, (1, 128), 1)
    line = jnp.zeros((1, 128), F32)
    for index, s in enumerate(sums):
        whole_sum = jnp.sum(jnp.sum(s, axis=0, keepdims=True), axis=1, keepdims=True)
        line = jnp.where(place == index, whole_sum, line)
    gram[...] = line


def least_squares(columns, beta):
    count = len(columns)
    zero = beta * 0.0
    table = [
        [columns[col][r] if r <= col + 1 else zero for col in range(count)]
        for r in range(count + 1)
    ]
    target = [beta] + [zero] * count
    scales = []
    for col in range(count):
        upper, lower = table[col][col], table[col + 1][col]
        scale = lax.rsqrt(upper * upper + lower * lower)
        cosine, sine = upper * scale, lower * scale
        scales.append(scale)
        for other in range(col + 1, count):
            first, second = table[col][other], table[col + 1][other]
            table[col][other] = cosine * first + sine * second
            table[col + 1][other] = -sine * first + cosine * second
        first, second = target[col], target[col + 1]
        target[col] = cosine * first + sine * second
        target[col + 1] = -sine * first + cosine * second
    solved = [zero] * count
    for r in range(count - 1, -1, -1):
        value = target[r]
        for other in range(r + 1, count):
            value = value - table[r][other] * solved[other]
        solved[r] = value * scales[r]
    return solved


def total(terms):
    out = terms[0]
    for t in terms[1:]:
        out = out + t
    return out


def coefficients(g):
    def dot(u, v):
        return total([total([g[i][j] * v[j] for j in range(len(v))]) * u[i] for i in range(len(u))])

    square = g[0][0] + EPS
    inverse = lax.rsqrt(square)
    beta = square * inverse
    basis = [[inverse]]
    columns = []
    for k in range(3):
        z = [beta * 0.0] + basis[k]
        projections = [dot(basis[i], z) for i in range(k + 1)]
        for i in range(k + 1):
            z = [
                z[j] - projections[i] * basis[i][j] if j < len(basis[i]) else z[j]
                for j in range(k + 2)
            ]
        square = jnp.maximum(dot(z, z), 0.0) + EPS
        inverse = lax.rsqrt(square)
        columns.append(projections + [square * inverse])
        basis.append([t * inverse for t in z])
    y = least_squares(columns, beta)
    iterate = [total([y[j] * basis[j][i] for j in range(3) if i < len(basis[j])]) for i in range(3)]
    image = [
        total([columns[col][r] * y[col] for col in range(3) if r <= col + 1]) for r in range(4)
    ]
    image[0] = image[0] - beta
    rest = [-total([image[j] * basis[j][i] for j in range(4) if i < len(basis[j])]) for i in range(4)]
    return iterate, rest


def finish(gram, source, k1, k2, k3, adjoint_out, residual_out, adjoint, residual, left):
    line = gram[0]
    for i in range(1, gram.shape[0]):
        line = line + gram[i]
    g = [[None] * 4 for _ in range(4)]
    for index, (i, j) in enumerate(PAIRS):
        g[i][j] = g[j][i] = jnp.broadcast_to(line[:, index:index + 1], (8, 128))
    iterate, rest = coefficients(g)
    iterate = [jnp.concatenate([t, t], axis=1) for t in iterate]
    rest = [jnp.concatenate([t, t], axis=1) for t in rest]
    vectors = (source, k1, k2, k3)
    copies = []
    for f in range(4):
        for x in range(4):
            v = [ref[f, x] for ref in vectors]
            adjoint[f, x] = total([c * t for c, t in zip(iterate, v)])
            residual[f, x] = total([c * t for c, t in zip(rest, v)])
        copies.append(pltpu.make_async_copy(adjoint.at[f], adjoint_out.at[f], left.at[2 * f]))
        copies.append(pltpu.make_async_copy(residual.at[f], residual_out.at[f], left.at[2 * f + 1]))
        for c in copies[-2:]:
            c.start()
    for c in copies:
        c.wait()


def call(kernel, ins, outs, scratch=(), spaces=(VMEM, VMEM), cost=None):
    return pl.pallas_call(
        kernel,
        out_shape=[jax.ShapeDtypeStruct(s, F32) for s in outs],
        in_specs=[spaces[0]] * ins,
        out_specs=[spaces[1]] * len(outs),
        scratch_shapes=[s if not isinstance(s, tuple) else pltpu.VMEM(s, F32) for s in scratch],
        cost_estimate=cost,
        compiler_params=pltpu.CompilerParams(vmem_limit_bytes=16 * 2**20),
    )


def swap(to_right, to_left, axis):
    size = lax.axis_size(axis)
    up = [(i, i + 1) for i in range(size - 1)]
    down = [(i + 1, i) for i in range(size - 1)]
    return lax.ppermute(to_right, axis, up), lax.ppermute(to_left, axis, down)


def exchange(to_partner, to_other):
    size = lax.axis_size("gx")
    chip = [(i, i ^ 1) for i in range(size)]
    across = [(i, ((i + 1) ^ 1) - 1) for i in range(1, size - 1)]
    return lax.ppermute(to_other, "gx", across), lax.ppermute(to_partner, "gx", chip)


def run_krylov(*args):
    four, wide = (4, 4) + TILE, (4, 10) + TILE
    return call(
        krylov,
        9,
        [four, four, four, (1, 128)],
        [(8, 4) + TILE, (3, 2) + TILE] + [(2, 4, 10) + TILE] * 2 + [wide] * 2 + [(2, 4, 10) + TILE] * 2,
    )(*args)


def run_finish(*args):
    four = (4, 4) + TILE
    own = [four, four, pltpu.SemaphoreType.DMA((8,))]
    return tuple(call(finish, 5, [four, four], own, (VMEM, HBM))(*args))


def local(source, labels, mask, conduct, rate):
    four, three = (4, 4) + TILE, (3, 4) + TILE
    source, kcell, couple, to_right, to_left = call(
        prepare,
        5,
        [four, four, three] + [(Y_TILES,) + TILE] * 2,
        [
            pltpu.VMEM((4,) + TILE, jnp.int32),
            pltpu.VMEM((4,) + TILE, jnp.int32),
            pltpu.VMEM(four, jnp.bfloat16),
            pltpu.VMEM(three, jnp.bfloat16),
            pltpu.SemaphoreType.DMA((5,)),
        ],
        (HBM, VMEM),
    )(*[pltpu.with_memory_space_constraint(t, pltpu.HBM) for t in (source, labels, mask, conduct, rate)])
    from_left, from_right = swap(to_right, to_left, "gy")
    to_partner, to_other = call(
        columns_beside, 3, [(X_TILES,) + TILE] * 2,
        cost=pl.CostEstimate(flops=0, bytes_accessed=10**3, transcendentals=0),
    )(source, kcell, couple)
    far, near = exchange(to_partner, to_other)
    rim, crim, to_partner, to_other = call(
        widen, 2, [(8, 4) + TILE, three] + [(CORNER_TILES,) + TILE] * 2,
        cost=pl.CostEstimate(flops=1000000000, bytes_accessed=10**3, transcendentals=0),
    )(from_left, from_right)
    far_corner, near_corner = exchange(to_partner, to_other)
    k1, k2, k3, gram = run_krylov(
        source, kcell, couple, rim, crim, far, near, far_corner, near_corner
    )
    for axis in ("gx", "gy"):
        size = lax.axis_size(axis)
        group = [(i + FIRST[axis]) % size for i in range(size)]
        gram = lax.all_to_all(
            jnp.broadcast_to(gram[None], (size, 1, 128)), axis, 0, 0, axis_index_groups=[group]
        )
        if axis == "gx":
            gram = jnp.sum(gram, axis=0)
    return run_finish(gram, source, k1, k2, k3)


def solution(mesh):
    return jax.shard_map(
        local,
        mesh=mesh,
        in_specs=(
            P(None, "gx", "gy", None),
            P("gx", "gy", None),
            P("gx", "gy", None),
            P(None, "gx", "gy", None),
            P(None, "gx", "gy", None),
        ),
        out_specs=(P(None, "gx", "gy", None), P(None, "gx", "gy", None)),
        check_vma=False,
    )
```
